128 devices in a mesh: lon: 16 (over y, x_lo, core), lat: 8 (over z, x_hi).
Axes of the slice: x: 4 (x_hi: 2, x_lo: 2; x = x_hi * 2 + x_lo), y: 4, z: 4, core: 2. Of those that a mesh axis runs over, the one named last changes fastest.
Arguments:
- queries: bfloat16 [8, 32, 64, 1024], P('lat', 'lon'), may hold values from -6 to 6
- keys: bfloat16 [8, 32, 64, 1024], P('lat', 'lon'), may hold values from -6 to 6
- values: bfloat16 [8, 32, 64, 1024], P('lat', 'lon'), may hold values from -6 to 6
- season: bfloat16 [8, 32, 64, 1024], P('lat', 'lon'), may hold values from -6 to 6
- cloud: int32 [8, 32], replicated, may hold values 0 or 1
- pairing: int32 [8, 32, 64], P('lat', 'lon'), may hold values from 0 to 63
Outputs:
- loss_map: float32 [8, 32, 64], P('lat', 'lon')
- query_grad: bfloat16 [8, 32, 64, 1024], P('lat', 'lon')
- key_grad: bfloat16 [8, 32, 64, 1024], P('lat', 'lon')
- value_grad: bfloat16 [8, 32, 64, 1024], P('lat', 'lon')
The draws below stay inside these ranges and needn't reach their ends.
All inputs are finite; a program needn't handle non-finite values.
Results may differ from the reference program's by a relative error of at most 0.017.
The reference program's roundings to bfloat16 on the way count: a program that leaves them out, or rounds other values in their place, can miss the bound.
Values may be sent and summed in bfloat16 or wider, within the bound.
No kernel may reach another device: no remote copies, remote signals or barrier semaphores. Data moves between devices by JAX's collectives and lax.ppermute only.
A program may use at most 128 MiB of HBM per device.

```python
import jax
import jax.numpy as jnp
from jax import lax

HEADS = 16
HDIM = 64
PP = 64
LATB = 8
LONB = 32


def draw_all(key):
    shape = (LATB, LONB, PP, HEADS * HDIM)
    query_draw = jnp.clip(jax.random.normal(jax.random.fold_in(key, 21), shape), -6.0, 6.0)
    key_draw = jnp.clip(jax.random.normal(jax.random.fold_in(key, 22), shape), -6.0, 6.0)
    value_draw = jnp.clip(jax.random.normal(jax.random.fold_in(key, 23), shape), -6.0, 6.0)
    season_draw = jnp.clip(jax.random.normal(jax.random.fold_in(key, 24), shape), -6.0, 6.0)
    return (query_draw, key_draw, value_draw, season_draw)


def draw_queries(key, part):
    return draw_all(key)[0].astype(jnp.bfloat16)


def draw_keys(key, part):
    return draw_all(key)[1].astype(jnp.bfloat16)


def draw_values(key, part):
    return draw_all(key)[2].astype(jnp.bfloat16)


def draw_season(key, part):
    return draw_all(key)[3].astype(jnp.bfloat16)


def place_ends(entries, stream_key, least, high):
    spot = [jax.random.randint(jax.random.fold_in(stream_key, axis), (), 0, length) for axis, length in enumerate(entries.shape)]
    widest = entries.shape.index(max(entries.shape))
    neighbour = spot[:widest] + [(spot[widest] + 1) % entries.shape[widest]] + spot[widest + 1:]
    return entries.at[tuple(spot)].set(least).at[tuple(neighbour)].set(high)


def setup_inputs(seed: int = 0) -> dict:
    key_list = jax.random.split(jax.random.key(seed), 7)
    queries = draw_queries(jax.random.fold_in(key_list[6], 71), 0)
    keys = draw_keys(jax.random.fold_in(key_list[6], 71), 0)
    values = draw_values(jax.random.fold_in(key_list[6], 71), 0)
    season = draw_season(jax.random.fold_in(key_list[6], 71), 0)
    cloud = place_ends((jax.random.randint(key_list[4], (LATB, LONB), 0, 4) < 3).astype(jnp.int32), jax.random.fold_in(key_list[4], 1), 0, 1)
    pairing = place_ends(jax.random.randint(key_list[5], (LATB, LONB, PP), 0, PP), jax.random.fold_in(key_list[5], 1), 0, PP - 1).astype(jnp.int32)
    return dict(queries=queries, keys=keys, values=values, season=season, cloud=cloud, pairing=pairing)


NEG_FILL = -1.0e30


def offsets():
    return [(lat_step, lon_step) for lat_step in (-1, 0, 1) for lon_step in (-1, 0, 1)]


def allowed_table(cloud):
    grid_rows = cloud.shape[0]
    row_ids = jnp.arange(grid_rows, dtype=jnp.int32)[:, None]
    columns = []
    for lat_step, lon_step in offsets():
        inside = (row_ids + lat_step >= 0) & (row_ids + lat_step < grid_rows)
        shifted = jnp.roll(cloud, (-lat_step, -lon_step), axis=(0, 1))
        if lat_step == 0 and lon_step == 0:
            usable = jnp.ones(cloud.shape, dtype=jnp.bool_)
        else:
            usable = shifted == 1
        columns.append(inside & usable)
    return jnp.stack(columns, axis=-1)


def key_table(cloud):
    grid_rows = cloud.shape[0]
    row_ids = jnp.arange(grid_rows, dtype=jnp.int32)[:, None]
    columns = []
    for lat_step, lon_step in offsets():
        inside = (row_ids + lat_step >= 0) & (row_ids + lat_step < grid_rows)
        if lat_step == 0 and lon_step == 0:
            usable = jnp.ones(cloud.shape, dtype=jnp.bool_)
        else:
            usable = cloud == 1
        columns.append(inside & usable)
    return jnp.stack(columns, axis=-1)


def extend(array):
    array = jnp.concatenate([array[:, -1:], array, array[:, :1]], axis=1)
    padding = jnp.zeros((1,) + array.shape[1:], array.dtype)
    return jnp.concatenate([padding, array, padding], axis=0)


def window(extended, row_index, block_cols):
    pieces = []
    for lat_step, lon_step in offsets():
        lat_line = lax.dynamic_index_in_dim(extended, row_index + 1 + lat_step, 0, keepdims=False)
        pieces.append(lat_line[1 + lon_step:1 + lon_step + block_cols])
    return jnp.stack(pieces, axis=1)


def rounded(array):
    return lax.optimization_barrier(array.astype(jnp.bfloat16)).astype(jnp.float32)


def split_heads(array, rows_total, head_count):
    return array.reshape(array.shape[0], rows_total, head_count, -1).astype(jnp.float32)


def attend(query, key_win, value_win, opened, head_count):
    block_cols, patches, width = query.shape
    head_size = width // head_count
    query_heads = split_heads(query, patches, head_count)
    key_heads = split_heads(key_win, 9 * patches, head_count)
    value_heads = split_heads(value_win, 9 * patches, head_count)
    scores = jnp.einsum("bqhd,bkhd->bhqk", query_heads, key_heads) * head_size ** -0.5
    key_mask = jnp.repeat(opened, patches, axis=1)[:, None, None, :]
    scores = jnp.where(key_mask, scores, NEG_FILL)
    highest = jnp.max(scores, axis=-1, keepdims=True)
    log_total = highest + jnp.log(jnp.sum(jnp.exp(scores - highest), axis=-1, keepdims=True))
    attn_weights = rounded(jnp.exp(scores - log_total))
    attention_output = jnp.einsum("bhqk,bkhd->bqhd", attn_weights, value_heads)
    return attention_output.reshape(block_cols, patches, width).astype(jnp.bfloat16), log_total[..., 0]


def contrast(attention_output, season_window, opened, pair_row):
    block_cols, patches, width = attention_output.shape
    season_flattened = season_window.reshape(block_cols, 9 * patches, width).astype(jnp.float32)
    similarity_scores = jnp.einsum("cmu,cju->cmj", attention_output.astype(jnp.float32), season_flattened)
    key_mask = jnp.repeat(opened, patches, axis=1)[:, None, :]
    similarity_scores = jnp.where(key_mask, similarity_scores, NEG_FILL)
    highest = jnp.max(similarity_scores, axis=-1, keepdims=True)
    contrast_total = highest + jnp.log(jnp.sum(jnp.exp(similarity_scores - highest), axis=-1, keepdims=True))
    positive_indicator = pair_row[..., None] == jnp.arange(patches, dtype=jnp.int32)
    chosen = jnp.sum(jnp.where(positive_indicator, similarity_scores[:, :, 4 * patches:5 * patches], 0.0), axis=-1)
    loss_row = contrast_total[..., 0] - chosen
    contrastive_weight_table = rounded(jnp.exp(similarity_scores - contrast_total))
    gathered_neighbours = jnp.einsum("cim,cmo->cio", contrastive_weight_table, season_flattened)
    matching_pair = jnp.einsum("yga,yar->ygr", positive_indicator.astype(jnp.float32), season_window[:, 4].astype(jnp.float32))
    return loss_row, (gathered_neighbours - matching_pair).astype(jnp.bfloat16)


def row_delta(attention_output, attended_grad, head_count):
    block_cols, patches, width = attention_output.shape
    product = attention_output.astype(jnp.float32) * attended_grad.astype(jnp.float32)
    summed = jnp.sum(product.reshape(block_cols, patches, head_count, width // head_count), axis=-1)
    return jnp.transpose(summed, (0, 2, 1))


def query_grads(query, key_win, value_win, opened, log_total, deltas, attended_grad, head_count):
    block_cols, patches, width = query.shape
    head_size = width // head_count
    query_heads = split_heads(query, patches, head_count)
    key_heads = split_heads(key_win, 9 * patches, head_count)
    value_heads = split_heads(value_win, 9 * patches, head_count)
    grad_heads = split_heads(attended_grad, patches, head_count)
    scores = jnp.einsum("bqhd,bkhd->bhqk", query_heads, key_heads) * head_size ** -0.5
    key_mask = jnp.repeat(opened, patches, axis=1)[:, None, None, :]
    scores = jnp.where(key_mask, scores, NEG_FILL)
    attn_prob = jnp.exp(scores - log_total[..., None])
    grad_dot = jnp.einsum("bqhd,bkhd->bhqk", grad_heads, value_heads)
    score_grad = rounded(attn_prob * (grad_dot - deltas[..., None]))
    result = jnp.einsum("bhqk,bkhd->bqhd", score_grad, key_heads) * head_size ** -0.5
    return result.reshape(block_cols, patches, width).astype(jnp.bfloat16)


def key_grads(key_block, value_block, query_win, grad_win, total_win, delta_win, opened, head_count):
    block_cols, patches, width = key_block.shape
    head_size = width // head_count
    query_heads = split_heads(query_win, 9 * patches, head_count)
    grad_heads = split_heads(grad_win, 9 * patches, head_count)
    key_heads = split_heads(key_block, patches, head_count)
    value_heads = split_heads(value_block, patches, head_count)
    scores = jnp.einsum("bqhd,bkhd->bhqk", query_heads, key_heads) * head_size ** -0.5
    totals = jnp.transpose(total_win, (0, 2, 1, 3)).reshape(block_cols, head_count, 9 * patches)
    deltas = jnp.transpose(delta_win, (0, 2, 1, 3)).reshape(block_cols, head_count, 9 * patches)
    query_mask = jnp.repeat(opened, patches, axis=1)[:, None, :, None]
    attn_prob = jnp.where(query_mask, jnp.exp(scores - totals[..., None]), 0.0)
    attn_weights = rounded(attn_prob)
    grad_dot = jnp.einsum("bqhd,bkhd->bhqk", grad_heads, value_heads)
    score_grad = rounded(attn_prob * (grad_dot - deltas[..., None]))
    key_result = jnp.einsum("bhqk,bqhd->bkhd", score_grad, query_heads) * head_size ** -0.5
    value_result = jnp.einsum("bhqk,bqhd->bkhd", attn_weights, grad_heads)
    return (key_result.reshape(block_cols, patches, width).astype(jnp.bfloat16),
            value_result.reshape(block_cols, patches, width).astype(jnp.bfloat16))


def reference(queries, keys, values, season, cloud, pairing):
    grid_rows, grid_cols, patches, width = queries.shape
    head_count = HEADS
    query_open = allowed_table(cloud)
    key_open = key_table(cloud)
    key_ext = extend(keys)
    value_ext = extend(values)
    season_ext = extend(season)
    row_list = jnp.arange(grid_rows, dtype=jnp.int32)

    def forward_row(row_index):
        opened = query_open[row_index]
        attention_output, log_total = attend(queries[row_index], window(key_ext, row_index, grid_cols),
                                     window(value_ext, row_index, grid_cols), opened, head_count)
        loss_row, grad_row = contrast(attention_output, window(season_ext, row_index, grid_cols), opened, pairing[row_index])
        return loss_row, grad_row, log_total, row_delta(attention_output, grad_row, head_count)

    loss_map, attended_grad, log_total, deltas = lax.map(forward_row, row_list)

    def query_row(row_index):
        return query_grads(queries[row_index], window(key_ext, row_index, grid_cols),
                           window(value_ext, row_index, grid_cols), query_open[row_index],
                           log_total[row_index], deltas[row_index], attended_grad[row_index], head_count)

    query_grad = lax.map(query_row, row_list)
    query_ext = extend(queries)
    grad_ext = extend(attended_grad)
    stats_ext = extend(jnp.stack([log_total, deltas], axis=2))

    def key_row(row_index):
        stats_win = window(stats_ext, row_index, grid_cols)
        return key_grads(keys[row_index], values[row_index], window(query_ext, row_index, grid_cols),
                         window(grad_ext, row_index, grid_cols), stats_win[:, :, 0], stats_win[:, :, 1],
                         key_open[row_index], head_count)

    key_grad, value_grad = lax.map(key_row, row_list)
    return loss_map, query_grad, key_grad, value_grad
```

```python
import functools

import jax
import jax.numpy as jnp
from jax import lax
from jax.experimental import pallas as pl
from jax.experimental.pallas import tpu as pltpu
from jax.sharding import PartitionSpec as P

HEADS = 16
HDIM = 64
PP = 64
WIDTH = HEADS * HDIM
GROUP = 4
GW = GROUP * HDIM
GROUPS = HEADS // GROUP
ROWS = GROUP * PP
WIN = 9 * PP
REG = 12 * PP
EXT = WIDTH + 128
NEG_FILL = -1e30
SCALE = HDIM ** -0.5
AXES = ("lon", "lat")
VMEM_LIMIT = 48 * 1024 * 1024
BF = jnp.bfloat16
F32 = jnp.float32

NT = (((1,), (1,)), ((), ()))
NN = (((1,), (0,)), ((), ()))


def dot(a, b, dims):
    return lax.dot_general(a, b, dims, preferred_element_type=F32)


def routes(rows, cols):
    def at(r, c):
        return (c % cols) * rows + r

    cells = [(r, c) for r in range(rows) for c in range(cols)]

    def away(c):
        return c + 1 if c % 2 else c - 1

    def hop(r):
        return r + 2 if r % 2 == 0 else r - 2

    return dict(
        swap=[(at(r, c), at(r ^ 1, c)) for r, c in cells],
        off=[(at(r, c), at(r, away(c))) for r, c in cells],
        cor=[(at(r, c), at(r ^ 1, away(c))) for r, c in cells],
        far=[(at(r, c), at(hop(r), c)) for r, c in cells if 0 <= hop(r) < rows],
        twin=[(at(r, c), at(r, c ^ 1)) for r, c in cells],
    )


def exchange(own, near, face_of, way):
    swap = lax.ppermute(own, AXES, way["swap"])
    off = lax.ppermute(near, AXES, way["off"])
    cor = lax.ppermute(near, AXES, way["cor"])
    far = lax.ppermute(jnp.concatenate([swap, cor], axis=0), AXES, way["far"])
    facing = jnp.concatenate([face_of(own), face_of(swap), face_of(far)], axis=0)
    twin = lax.ppermute(facing, AXES, way["twin"])
    return (own, swap, far, off, cor, twin)


def region_piece(pieces, n, row, col):
    own, swap, far, off, cor, twin = pieces
    if col == 0:
        return (off.at[0], cor.at[0], far.at[2])[row]
    if col == 3:
        return twin.at[row]
    base = (own, swap, far)[row]
    return base.at[n if col == 1 else 1 - n]


def window_copies(pieces, n, dst, sems, first):
    out = []
    for t in range(2):
        mine = []
        for row in range(3):
            for col in range(3):
                slot = row * 3 + col
                mine.append(
                    pltpu.make_async_copy(
                        region_piece(pieces, n, row, col + t),
                        dst.at[t, pl.ds(slot * PP, PP), :],
                        sems.at[first + t * 9 + slot],
                    )
                )
        out.append(mine)
    return out


def begin(copies):
    for c in copies:
        c.start()


def finish(copies):
    for c in copies:
        c.wait()


def spread(x):
    lane = lax.broadcasted_iota(jnp.int32, x.shape, 1) // HDIM
    return jnp.concatenate([jnp.where(lane == h, x, jnp.zeros_like(x)) for h in range(GROUP)], axis=0)


def gather_heads(y):
    lane = lax.broadcasted_iota(jnp.int32, (PP, GW), 1) // HDIM
    out = y[0:PP]
    for h in range(1, GROUP):
        out = jnp.where(lane == h, y[h * PP : (h + 1) * PP], out)
    return out


def group_slice(g):
    return pl.ds(pl.multiple_of(g * GW, GW), GW)


def attend_kernel(n_ref, q_ref, mask_ref, *rest):
    k_pieces, v_pieces = rest[0:6], rest[6:12]
    att_ref, stat_ref, k9, v9, sems = rest[12:]
    n = n_ref[0]
    kc = window_copies(k_pieces, n, k9, sems, 0)
    vc = window_copies(v_pieces, n, v9, sems, 18)
    for t in range(2):
        begin(kc[t])
        begin(vc[t])
    for t in range(2):
        finish(kc[t])
        finish(vc[t])
        qt = n if t == 0 else 1 - n
        stat_ref[t] = jnp.zeros((PP, 128), F32)

        def step(g, carry):
            fs = group_slice(g)
            q = spread(q_ref[qt, :, fs] * SCALE)
            s = dot(q, k9[t, :, fs], NT) + mask_ref[t : t + 1, :]
            m = jnp.max(s, axis=1, keepdims=True)
            e = jnp.exp(s - m)
            total = jnp.sum(e, axis=1, keepdims=True)
            p = (e * (1.0 / total)).astype(BF)
            lse = m + jnp.log(total)
            att_ref[t, :, fs] = gather_heads(dot(p, v9[t, :, fs], NN)).astype(BF)
            lane = lax.broadcasted_iota(jnp.int32, (PP, 128), 1)
            stat = stat_ref[t]
            for h in range(GROUP):
                stat = jnp.where(lane == g * GROUP + h, lse[h * PP : (h + 1) * PP], stat)
            stat_ref[t] = stat
            return carry

        lax.fori_loop(0, GROUPS, step, 0)


def contrast_kernel(n_ref, att_ref, stat_ref, mask_ref, pos_ref, *rest):
    pieces = rest[0:6]
    loss_ref, grad_ref, stats_ref, s12, sems = rest[6:]
    n = n_ref[0]
    copies = []
    for row in range(3):
        for col in range(4):
            slot = row * 4 + col
            copies.append(
                pltpu.make_async_copy(
                    region_piece(pieces, n, row, col), s12.at[pl.ds(slot * PP, PP), :], sems.at[slot]
                )
            )
    begin(copies)
    finish(copies)
    att = jnp.concatenate([att_ref[0], att_ref[1]], axis=0)
    side = lax.broadcasted_iota(jnp.int32, (2 * PP, REG), 0) < PP
    mask = jnp.where(side, mask_ref[0:1, :], mask_ref[1:2, :])
    logits = dot(att, s12[...], NT) + mask
    m = jnp.max(logits, axis=1, keepdims=True)
    e = jnp.exp(logits - m)
    total = jnp.sum(e, axis=1, keepdims=True)
    w = (e * (1.0 / total)).astype(BF)
    ctotal = m + jnp.log(total)
    pos = pos_ref[...]
    hit = lax.broadcasted_iota(jnp.int32, (2 * PP, 4 * PP), 1) == pos
    chosen = jnp.sum(jnp.where(hit, logits[:, 0 : 4 * PP], 0.0), axis=1, keepdims=True)
    loss_ref[...] = ctotal - chosen
    acc = dot(w, s12[...], NN) - dot(hit.astype(F32).astype(BF), s12[0 : 4 * PP, :], NN)
    grad = acc.astype(BF)
    prod = grad.astype(F32) * att.astype(F32)
    high = prod.astype(BF)
    low = (prod - high.astype(F32)).astype(BF)
    feat = lax.broadcasted_iota(jnp.int32, (WIDTH, 128), 0) // HDIM
    lane = lax.broadcasted_iota(jnp.int32, (WIDTH, 128), 1)
    pick = (lane == feat + HEADS).astype(F32).astype(BF)
    delta = dot(high, pick, NN) + dot(low, pick, NN)
    stat = jnp.concatenate([stat_ref[0], stat_ref[1]], axis=0) + delta
    part0 = stat.astype(BF).astype(F32)
    part1 = (stat - part0).astype(BF).astype(F32)
    part2 = (stat - part0 - part1).astype(BF).astype(F32)
    packed = part0 + pltpu.roll(part1, 32, 1) + pltpu.roll(part2, 64, 1)
    packed = packed.astype(BF)
    for t in range(2):
        rows = slice(t * PP, (t + 1) * PP)
        grad_ref[t, :, 0:WIDTH] = grad[rows]
        grad_ref[t, :, WIDTH:EXT] = packed[rows]
        stats_ref[t] = stat[rows]


def head_column(stat, index):
    lane = lax.broadcasted_iota(jnp.int32, (PP, 128), 1)
    cols = [
        jnp.sum(jnp.where(lane == index + h, stat, 0.0), axis=1, keepdims=True) for h in range(GROUP)
    ]
    return jnp.concatenate(cols, axis=0)


def query_kernel(n_ref, q_ref, grad_ref, stats_ref, mask_ref, *rest):
    k_pieces, v_pieces = rest[0:6], rest[6:12]
    out_ref, k9, v9, sems = rest[12:]
    n = n_ref[0]
    kc = window_copies(k_pieces, n, k9, sems, 0)
    vc = window_copies(v_pieces, n, v9, sems, 18)
    for t in range(2):
        begin(kc[t])
        begin(vc[t])
    for t in range(2):
        finish(kc[t])
        finish(vc[t])
        qt = n if t == 0 else 1 - n

        def step(g, carry):
            fs = group_slice(g)
            q = spread(q_ref[qt, :, fs] * SCALE)
            stat = stats_ref[t]
            lse = head_column(stat, g * GROUP)
            delta = head_column(stat, g * GROUP + HEADS)
            s = dot(q, k9[t, :, fs], NT) + mask_ref[t : t + 1, :]
            p = jnp.exp(s - lse)
            gd = dot(spread(grad_ref[t, :, fs]), v9[t, :, fs], NT)
            ds = (p * (gd - delta)).astype(BF)
            out = gather_heads(dot(ds, k9[t, :, fs], NN)) * SCALE
            out_ref[qt, :, fs] = out.astype(BF)
            return carry

        lax.fori_loop(0, GROUPS, step, 0)


def key_kernel(n_ref, k_ref, v_ref, mask_ref, *rest):
    q_pieces, g_pieces = rest[0:6], rest[6:12]
    kout_ref, vout_ref, q9, g9, rows_ref, sems = rest[12:]
    n = n_ref[0]
    qc = window_copies(q_pieces, n, q9, sems, 0)
    gc = window_copies(g_pieces, 0, g9, sems, 18)
    for t in range(2):
        begin(qc[t])
        begin(gc[t])
    for t in range(2):
        finish(qc[t])
        finish(gc[t])
        kt = n if t == 0 else 1 - n
        parts = jnp.transpose(g9[t, :, WIDTH:EXT].astype(F32))
        stats = parts[0:32] + parts[32:64] + parts[64:96]
        rows_ref[0:HEADS] = stats[0:HEADS] + mask_ref[t : t + 1, :]
        rows_ref[HEADS : 2 * HEADS] = stats[HEADS : 2 * HEADS]

        def step(g, carry):
            fs = group_slice(g)
            ks = spread(k_ref[kt, :, fs] * SCALE)
            vs = spread(v_ref[kt, :, fs])
            qw = q9[t, :, fs]
            gw = g9[t, :, fs]
            s = dot(ks, qw, NT)
            gd = dot(vs, gw, NT)
            ps, dss = [], []
            for h in range(GROUP):
                part = slice(h * PP, (h + 1) * PP)
                lse = rows_ref[pl.ds(g * GROUP + h, 1), :]
                delta = rows_ref[pl.ds(HEADS + g * GROUP + h, 1), :]
                p = jnp.exp(s[part] - lse)
                ps.append(p.astype(BF))
                dss.append((p * (gd[part] - delta)).astype(BF))
            p = jnp.concatenate(ps, axis=0)
            ds = jnp.concatenate(dss, axis=0)
            kout_ref[kt, :, fs] = (gather_heads(dot(ds, qw, NN)) * SCALE).astype(BF)
            vout_ref[kt, :, fs] = gather_heads(dot(p, gw, NN)).astype(BF)
            return carry

        lax.fori_loop(0, GROUPS, step, 0)


SMEM = pl.BlockSpec(memory_space=pltpu.SMEM)
VMEM = pl.BlockSpec(memory_space=pltpu.VMEM)
ANY = pl.BlockSpec(memory_space=pl.ANY)


def call(kernel, name, in_specs, out_shape, scratch, flops):
    return pl.pallas_call(
        kernel,
        name=name,
        out_shape=out_shape,
        in_specs=in_specs,
        out_specs=jax.tree.map(lambda _: VMEM, out_shape),
        scratch_shapes=scratch,
        compiler_params=pltpu.CompilerParams(vmem_limit_bytes=VMEM_LIMIT),
        cost_estimate=pl.CostEstimate(flops=flops, bytes_accessed=6_000_000, transcendentals=0),
    )


def shape(dims, dtype):
    return jax.ShapeDtypeStruct(dims, dtype)


def body(way, queries, keys, values, season, cloud, pairing):
    grid_rows, grid_cols = cloud.shape
    lat = lax.axis_index("lat")
    lon = lax.axis_index("lon")
    odd = lon % 2
    q, k, v, s = (x[0] for x in (queries, keys, values, season))

    def near_of(x):
        return lax.dynamic_slice_in_dim(x, odd, 1, axis=0)

    def face_of(x):
        return lax.dynamic_slice_in_dim(x, 1 - odd, 1, axis=0)

    sign = 2 * odd - 1
    near_col = 2 * lon + odd
    reg_cols = jnp.stack([near_col + sign, near_col, near_col - sign, near_col - 2 * sign]) % grid_cols
    outer = jnp.where(lat % 2 == 0, lat - 1, lat + 1)
    reg_rows = jnp.stack([lat, lat ^ 1, outer])
    inside = (reg_rows >= 0) & (reg_rows < grid_rows)
    clear = cloud[jnp.clip(reg_rows, 0, grid_rows - 1)][:, reg_cols] == 1
    clear = clear & inside[:, None]
    itself = jnp.zeros((3, 3), jnp.bool_).at[0, 1].set(True)
    q_open = jnp.stack([clear[:, 0:3] | itself, clear[:, 1:4] | itself])
    pad = jnp.zeros((3, 1), jnp.bool_)
    c_open = jnp.stack(
        [jnp.concatenate([q_open[0], pad], axis=1), jnp.concatenate([pad, q_open[1]], axis=1)]
    )
    own_clear = jnp.stack([clear[0, 1], clear[0, 2]])
    k_open = (own_clear[:, None, None] & inside[None, :, None]) | itself[None]
    q_mask = jnp.where(jnp.repeat(q_open.reshape(2, 9), PP, axis=1), 0.0, NEG_FILL)
    c_mask = jnp.where(jnp.repeat(c_open.reshape(2, 12), PP, axis=1), 0.0, NEG_FILL)
    k_mask = jnp.where(jnp.repeat(k_open.reshape(2, 9), PP, axis=1), 0.0, -NEG_FILL)
    n = odd.astype(jnp.int32).reshape(1)
    pair = pairing[0]
    pair = jnp.where(odd == 1, pair[::-1], pair)
    pos = (pair + jnp.array([[PP], [2 * PP]], jnp.int32)).reshape(2 * PP, 1)

    kp = exchange(k, near_of(k), face_of, way)
    vp = exchange(v, near_of(v), face_of, way)
    sp = exchange(s, near_of(s), face_of, way)
    qp = exchange(q, near_of(q), face_of, way)

    att, stat = call(
        attend_kernel,
        "attend",
        [SMEM, VMEM, VMEM] + [ANY] * 12,
        (shape((2, PP, WIDTH), BF), shape((2, PP, 128), F32)),
        [pltpu.VMEM((2, WIN, WIDTH), BF)] * 2 + [pltpu.SemaphoreType.DMA((36,))],
        2_400_000_000,
    )(n, q, q_mask, *kp, *vp)

    loss, grad, stats = call(
        contrast_kernel,
        "contrast",
        [SMEM, VMEM, VMEM, VMEM, VMEM] + [ANY] * 6,
        (shape((2 * PP, 1), F32), shape((2, PP, EXT), BF), shape((2, PP, 128), F32)),
        [pltpu.VMEM((REG, WIDTH), BF), pltpu.SemaphoreType.DMA((12,))],
        1_200_000_000,
    )(n, att, stat, c_mask, pos, *sp)

    gp = exchange(grad, grad[0:1], lambda x: x[1:2], way)

    query_grad = call(
        query_kernel,
        "query_grads",
        [SMEM, VMEM, VMEM, VMEM, VMEM] + [ANY] * 12,
        shape((2, PP, WIDTH), BF),
        [pltpu.VMEM((2, WIN, WIDTH), BF)] * 2 + [pltpu.SemaphoreType.DMA((36,))],
        3_600_000_000,
    )(n, q, grad, stats, q_mask, *kp, *vp)

    key_grad, value_grad = call(
        key_kernel,
        "key_grads",
        [SMEM, VMEM, VMEM, VMEM] + [ANY] * 12,
        (shape((2, PP, WIDTH), BF), shape((2, PP, WIDTH), BF)),
        [
            pltpu.VMEM((2, WIN, WIDTH), BF),
            pltpu.VMEM((2, WIN, EXT), BF),
            pltpu.VMEM((2 * HEADS, WIN), F32),
            pltpu.SemaphoreType.DMA((36,)),
        ],
        4_800_000_000,
    )(n, k, v, k_mask, *qp, *gp)

    loss_map = loss.reshape(2, PP)
    loss_map = jnp.where(odd == 1, loss_map[::-1], loss_map)
    return (loss_map[None], query_grad[None], key_grad[None], value_grad[None])


def solution(mesh):
    block = P("lat", "lon", None, None)
    line = P("lat", "lon", None)
    way = routes(mesh.shape["lat"], mesh.shape["lon"])
    return jax.shard_map(
        functools.partial(body, way),
        mesh=mesh,
        in_specs=(block, block, block, block, P(), line),
        out_specs=(line, block, block, block),
        check_vma=False,
    )
```

```python
import functools

import jax
import jax.numpy as jnp
from jax import lax
from jax.experimental import pallas as pl
from jax.experimental.pallas import tpu as pltpu
from jax.sharding import PartitionSpec as P

HEADS = 16
HDIM = 64
PP = 64
WIDTH = HEADS * HDIM
GROUP = 4
GW = GROUP * HDIM
GROUPS = HEADS // GROUP
ROWS = GROUP * PP
WIN = 9 * PP
REG = 12 * PP
EXT = WIDTH + 128
NEG_FILL = -1e30
SCALE = HDIM ** -0.5
AXES = ("lon", "lat")
VMEM_LIMIT = 48 * 1024 * 1024
BF = jnp.bfloat16
F32 = jnp.float32

NT = (((1,), (1,)), ((), ()))
NN = (((1,), (0,)), ((), ()))


def dot(a, b, dims):
    return lax.dot_general(a, b, dims, preferred_element_type=F32)


def routes(rows, cols):
    def at(r, c):
        return (c % cols) * rows + r

    cells = [(r, c) for r in range(rows) for c in range(cols)]

    def away(c):
        return c + 1 if c % 2 else c - 1

    def hop(r):
        return r + 2 if r % 2 == 0 else r - 2

    return dict(
        swap=[(at(r, c), at(r ^ 1, c)) for r, c in cells],
        off=[(at(r, c), at(r, away(c))) for r, c in cells],
        cor=[(at(r, c), at(r ^ 1, away(c))) for r, c in cells],
        far=[(at(r, c), at(hop(r), c)) for r, c in cells if 0 <= hop(r) < rows],
        twin=[(at(r, c), at(r, c ^ 1)) for r, c in cells],
    )


def exchange(own, near, face_of, way):
    swap = lax.ppermute(own, AXES, way["swap"])
    off = lax.ppermute(near, AXES, way["off"])
    cor = lax.ppermute(near, AXES, way["cor"])
    far = lax.ppermute(jnp.concatenate([swap, cor], axis=0), AXES, way["far"])
    facing = jnp.concatenate([face_of(own), face_of(swap), face_of(far)], axis=0)
    twin = lax.ppermute(facing, AXES, way["twin"])
    return (own, swap, far, off, cor, twin)


def region_block(pieces, n, row, col, fs):
    own, swap, far, off, cor, twin = pieces
    if col == 0:
        ref, index = ((off, 0), (cor, 0), (far, 2))[row]
    elif col == 3:
        ref, index = twin, row
    else:
        ref, index = (own, swap, far)[row], n if col == 1 else 1 - n
    return ref[index, :, fs]


def window(pieces, n, t, fs):
    return jnp.concatenate(
        [region_block(pieces, n, row, col + t, fs) for row in range(3) for col in range(3)], axis=0
    )


def spread(x):
    lane = lax.broadcasted_iota(jnp.int32, x.shape, 1) // HDIM
    return jnp.concatenate([jnp.where(lane == h, x, jnp.zeros_like(x)) for h in range(GROUP)], axis=0)


def gather_heads(y):
    lane = lax.broadcasted_iota(jnp.int32, (PP, GW), 1) // HDIM
    out = y[0:PP]
    for h in range(1, GROUP):
        out = jnp.where(lane == h, y[h * PP : (h + 1) * PP], out)
    return out


def group_slice(g):
    return pl.ds(pl.multiple_of(g * GW, GW), GW)


def region_flags(here_ref, cloud_ref):
    rows, cols = cloud_ref.shape
    lat, lon = here_ref[0], here_ref[1]
    odd = lon % 2
    sign = 2 * odd - 1
    near = 2 * lon + odd
    outer = jnp.where(lat % 2 == 0, lat - 1, lat + 1)
    within = (outer >= 0) & (outer < rows)
    partner = jnp.where(lat % 2 == 0, lat + 1, lat - 1)
    lines = (lat, partner, jnp.clip(outer, 0, rows - 1))
    inside = (True, True, within)
    clear = []
    for row in range(3):
        line = []
        for col in range(4):
            c = (near + sign * (1 - col) + cols) % cols
            flag = cloud_ref[lines[row], c] == 1
            line.append(flag & within if row == 2 else flag)
        clear.append(line)
    return odd, inside, clear


def segments(flags, fill):
    width = PP * len(flags)
    slot = lax.broadcasted_iota(jnp.int32, (1, width), 1) // PP
    out = jnp.zeros((1, width), F32)
    for i, flag in enumerate(flags):
        if flag is not True:
            value = fill if flag is False else jnp.where(flag, 0.0, fill)
            out = jnp.where(slot == i, value, out)
    return out


def query_flags(clear, t):
    return [
        True if (row, col) == (0, 1) else clear[row][col + t] for row in range(3) for col in range(3)
    ]


def attend_kernel(here_ref, cloud_ref, q_ref, *rest):
    k_pieces, v_pieces = rest[0:6], rest[6:12]
    att_ref, stat_ref = rest[12:]
    n, _, clear = region_flags(here_ref, cloud_ref)
    for t in range(2):
        qt = n if t == 0 else 1 - n
        stat_ref[t] = jnp.zeros((PP, 128), F32)
        mask = segments(query_flags(clear, t), NEG_FILL)

        def step(g, carry):
            fs = group_slice(g)
            q = spread(q_ref[qt, :, fs] * SCALE)
            kw = window(k_pieces, n, t, fs)
            s = dot(q, kw, NT) + mask
            m = jnp.max(s, axis=1, keepdims=True)
            e = jnp.exp(s - m)
            total = jnp.sum(e, axis=1, keepdims=True)
            p = (e * (1.0 / total)).astype(BF)
            lse = m + jnp.log(total)
            att_ref[t, :, fs] = gather_heads(dot(p, window(v_pieces, n, t, fs), NN)).astype(BF)
            lane = lax.broadcasted_iota(jnp.int32, (PP, 128), 1)
            stat = stat_ref[t]
            for h in range(GROUP):
                stat = jnp.where(lane == g * GROUP + h, lse[h * PP : (h + 1) * PP], stat)
            stat_ref[t] = stat
            return carry

        lax.fori_loop(0, GROUPS, step, 0, unroll=True)


def contrast_kernel(here_ref, cloud_ref, att_ref, stat_ref, pair_ref, *rest):
    pieces = rest[0:6]
    loss_ref, grad_ref, stats_ref = rest[6:]
    n, _, clear = region_flags(here_ref, cloud_ref)
    whole = slice(0, WIDTH)
    season = jnp.concatenate(
        [region_block(pieces, n, row, col, whole) for row in range(3) for col in range(4)], axis=0
    )
    att = jnp.concatenate([att_ref[0], att_ref[1]], axis=0)
    side = lax.broadcasted_iota(jnp.int32, (2 * PP, REG), 0) < PP
    sides = []
    for t in range(2):
        flags = query_flags(clear, t)
        line = []
        for row in range(3):
            mine = flags[row * 3 : row * 3 + 3]
            line += mine + [False] if t == 0 else [False] + mine
        sides.append(segments(line, NEG_FILL))
    mask = jnp.where(side, sides[0], sides[1])
    logits = dot(att, season, NT) + mask
    m = jnp.max(logits, axis=1, keepdims=True)
    e = jnp.exp(logits - m)
    total = jnp.sum(e, axis=1, keepdims=True)
    w = (e * (1.0 / total)).astype(BF)
    ctotal = m + jnp.log(total)
    key = lax.broadcasted_iota(jnp.int32, (4 * PP, PP), 0)
    hits = []
    for t in range(2):
        pair = pair_ref[pl.ds(n if t == 0 else 1 - n, 1), :]
        hits.append((key == pair + (1 + t) * PP).astype(F32))
    hit = jnp.transpose(jnp.concatenate(hits, axis=1)) > 0.5
    chosen = jnp.sum(jnp.where(hit, logits[:, 0 : 4 * PP], 0.0), axis=1, keepdims=True)
    loss = jnp.transpose(jnp.broadcast_to(ctotal - chosen, (2 * PP, 128)))
    for t in range(2):
        loss_ref[pl.ds(n if t == 0 else 1 - n, 1), :] = loss[0:1, t * PP : (t + 1) * PP]
    acc = dot(w, season, NN) - dot(hit.astype(F32).astype(BF), season[0 : 4 * PP], NN)
    grad = acc.astype(BF)
    prod = grad.astype(F32) * att.astype(F32)
    high = prod.astype(BF)
    low = (prod - high.astype(F32)).astype(BF)
    feat = lax.broadcasted_iota(jnp.int32, (WIDTH, 128), 0) // HDIM
    lane = lax.broadcasted_iota(jnp.int32, (WIDTH, 128), 1)
    pick = (lane == feat + HEADS).astype(F32).astype(BF)
    delta = dot(high, pick, NN) + dot(low, pick, NN)
    stat = jnp.concatenate([stat_ref[0], stat_ref[1]], axis=0) + delta
    part0 = stat.astype(BF).astype(F32)
    part1 = (stat - part0).astype(BF).astype(F32)
    part2 = (stat - part0 - part1).astype(BF).astype(F32)
    packed = part0 + pltpu.roll(part1, 32, 1) + pltpu.roll(part2, 64, 1)
    packed = packed.astype(BF)
    for t in range(2):
        rows = slice(t * PP, (t + 1) * PP)
        grad_ref[t, :, 0:WIDTH] = grad[rows]
        grad_ref[t, :, WIDTH:EXT] = packed[rows]
        stats_ref[t] = stat[rows]


def head_column(stat, index):
    lane = lax.broadcasted_iota(jnp.int32, (PP, 128), 1)
    cols = [
        jnp.sum(jnp.where(lane == index + h, stat, 0.0), axis=1, keepdims=True) for h in range(GROUP)
    ]
    return jnp.concatenate(cols, axis=0)


def query_kernel(here_ref, cloud_ref, q_ref, grad_ref, stats_ref, *rest):
    k_pieces, v_pieces = rest[0:6], rest[6:12]
    out_ref = rest[12]
    n, _, clear = region_flags(here_ref, cloud_ref)
    for t in range(2):
        qt = n if t == 0 else 1 - n
        mask = segments(query_flags(clear, t), NEG_FILL)

        def step(g, carry):
            fs = group_slice(g)
            q = spread(q_ref[qt, :, fs] * SCALE)
            stat = stats_ref[t]
            lse = head_column(stat, g * GROUP)
            delta = head_column(stat, g * GROUP + HEADS)
            kw = window(k_pieces, n, t, fs)
            s = dot(q, kw, NT) + mask
            p = jnp.exp(s - lse)
            gd = dot(spread(grad_ref[t, :, fs]), window(v_pieces, n, t, fs), NT)
            ds = (p * (gd - delta)).astype(BF)
            out = gather_heads(dot(ds, kw, NN)) * SCALE
            out_ref[qt, :, fs] = out.astype(BF)
            return carry

        lax.fori_loop(0, GROUPS, step, 0, unroll=True)


def key_kernel(here_ref, cloud_ref, k_ref, v_ref, *rest):
    q_pieces, g_pieces = rest[0:6], rest[6:12]
    kout_ref, vout_ref, rows_ref = rest[12:]
    n, inside, clear = region_flags(here_ref, cloud_ref)
    for t in range(2):
        kt = n if t == 0 else 1 - n
        parts = jnp.transpose(window(g_pieces, 0, t, slice(WIDTH, EXT)).astype(F32))
        stats = parts[0:32] + parts[32:64] + parts[64:96]
        seen = clear[0][1 + t]
        flags = [
            True if (row, col) == (0, 1) else (seen & inside[2] if row == 2 else seen)
            for row in range(3)
            for col in range(3)
        ]
        rows_ref[0:HEADS] = stats[0:HEADS] + segments(flags, -NEG_FILL)
        rows_ref[HEADS : 2 * HEADS] = stats[HEADS : 2 * HEADS]

        def step(g, carry):
            fs = group_slice(g)
            ks = spread(k_ref[kt, :, fs] * SCALE)
            vs = spread(v_ref[kt, :, fs])
            qw = window(q_pieces, n, t, fs)
            gw = window(g_pieces, 0, t, fs)
            s = dot(ks, qw, NT)
            gd = dot(vs, gw, NT)
            ps, dss = [], []
            for h in range(GROUP):
                part = slice(h * PP, (h + 1) * PP)
                lse = rows_ref[pl.ds(g * GROUP + h, 1), :]
                delta = rows_ref[pl.ds(HEADS + g * GROUP + h, 1), :]
                p = jnp.exp(s[part] - lse)
                ps.append(p.astype(BF))
                dss.append((p * (gd[part] - delta)).astype(BF))
            p = jnp.concatenate(ps, axis=0)
            ds = jnp.concatenate(dss, axis=0)
            kout_ref[kt, :, fs] = (gather_heads(dot(ds, qw, NN)) * SCALE).astype(BF)
            vout_ref[kt, :, fs] = gather_heads(dot(p, gw, NN)).astype(BF)
            return carry

        lax.fori_loop(0, GROUPS, step, 0, unroll=True)


SMEM = pl.BlockSpec(memory_space=pltpu.SMEM)
VMEM = pl.BlockSpec(memory_space=pltpu.VMEM)


def call(kernel, name, in_specs, out_shape, scratch, flops):
    return pl.pallas_call(
        kernel,
        name=name,
        out_shape=out_shape,
        in_specs=in_specs,
        out_specs=jax.tree.map(lambda _: VMEM, out_shape),
        scratch_shapes=scratch,
        compiler_params=pltpu.CompilerParams(vmem_limit_bytes=VMEM_LIMIT),
        cost_estimate=pl.CostEstimate(flops=flops, bytes_accessed=6_000_000, transcendentals=0),
    )


def shape(dims, dtype):
    return jax.ShapeDtypeStruct(dims, dtype)


def body(way, queries, keys, values, season, cloud, pairing):
    lat = lax.axis_index("lat")
    lon = lax.axis_index("lon")
    odd = lon % 2
    q, k, v, s = (x[0] for x in (queries, keys, values, season))

    def near_of(x):
        return lax.dynamic_slice_in_dim(x, odd, 1, axis=0)

    def face_of(x):
        return lax.dynamic_slice_in_dim(x, 1 - odd, 1, axis=0)

    here = jnp.stack([lat, lon]).astype(jnp.int32)

    kp = exchange(k, near_of(k), face_of, way)
    vp = exchange(v, near_of(v), face_of, way)
    sp = exchange(s, near_of(s), face_of, way)
    qp = exchange(q, near_of(q), face_of, way)

    att, stat = call(
        attend_kernel,
        "attend",
        [SMEM, SMEM, VMEM] + [VMEM] * 12,
        (shape((2, PP, WIDTH), BF), shape((2, PP, 128), F32)),
        [],
        2_400_000_000,
    )(here, cloud, q, *kp, *vp)

    loss, grad, stats = call(
        contrast_kernel,
        "contrast",
        [SMEM, SMEM, VMEM, VMEM, VMEM] + [VMEM] * 6,
        (shape((2, PP), F32), shape((2, PP, EXT), BF), shape((2, PP, 128), F32)),
        [],
        1_200_000_000,
    )(here, cloud, att, stat, pairing[0], *sp)

    gp = exchange(grad, grad[0:1], lambda x: x[1:2], way)

    query_grad = call(
        query_kernel,
        "query_grads",
        [SMEM, SMEM, VMEM, VMEM, VMEM] + [VMEM] * 12,
        shape((2, PP, WIDTH), BF),
        [],
        3_600_000_000,
    )(here, cloud, q, grad, stats, *kp, *vp)

    key_grad, value_grad = call(
        key_kernel,
        "key_grads",
        [SMEM, SMEM, VMEM, VMEM] + [VMEM] * 12,
        (shape((2, PP, WIDTH), BF), shape((2, PP, WIDTH), BF)),
        [pltpu.VMEM((2 * HEADS, WIN), F32)],
        4_800_000_000,
    )(here, cloud, k, v, *qp, *gp)

    return (loss[None], query_grad[None], key_grad[None], value_grad[None])


def solution(mesh):
    block = P("lat", "lon", None, None)
    line = P("lat", "lon", None)
    way = routes(mesh.shape["lat"], mesh.shape["lon"])
    return jax.shard_map(
        functools.partial(body, way),
        mesh=mesh,
        in_specs=(block, block, block, block, P(), line),
        out_specs=(line, block, block, block),
        check_vma=False,
    )
```

```python
import functools

import jax
import jax.numpy as jnp
from jax import lax
from jax.experimental import pallas as pl
from jax.experimental.pallas import tpu as pltpu
from jax.sharding import PartitionSpec as P

HEADS = 16
HDIM = 64
PP = 64
WIDTH = HEADS * HDIM
GROUP = 4
GW = GROUP * HDIM
GROUPS = HEADS // GROUP
ROWS = GROUP * PP
WIN = 9 * PP
REG = 12 * PP
EXT = WIDTH + 128
NEG_FILL = -1e30
SCALE = HDIM ** -0.5
AXES = ("lon", "lat")
VMEM_LIMIT = 48 * 1024 * 1024
BF = jnp.bfloat16
F32 = jnp.float32

NT = (((1,), (1,)), ((), ()))
NN = (((1,), (0,)), ((), ()))


def dot(a, b, dims):
    return lax.dot_general(a, b, dims, preferred_element_type=F32)


def routes(rows, cols):
    def at(r, c):
        return (c % cols) * rows + r

    cells = [(r, c) for r in range(rows) for c in range(cols)]

    def away(c):
        return c + 1 if c % 2 else c - 1

    def hop(r):
        return r + 2 if r % 2 == 0 else r - 2

    def past(r):
        return r - 1 if r % 2 == 0 else r + 1

    return dict(
        swap=[(at(r, c), at(r ^ 1, c)) for r, c in cells],
        off=[(at(r, c), at(r, away(c))) for r, c in cells],
        cor=[(at(r, c), at(r ^ 1, away(c))) for r, c in cells],
        far=[(at(r, c), at(hop(r), c)) for r, c in cells if 0 <= hop(r) < rows],
        twin=[(at(r, c), at(r, c ^ 1)) for r, c in cells],
        out=[(at(r, c), at(past(r), c)) for r, c in cells if 0 <= past(r) < rows],
        edge=[(at(r, c), at(past(r), away(c))) for r, c in cells if 0 <= past(r) < rows],
    )


def after(x, *done):
    return lax.optimization_barrier((x,) + done)[0]


def phase(*values):
    return lax.optimization_barrier(values)


def region(own, swap, far, off, cor, twins, n, side=0, inner=(0, 1, 2), corner=None):
    far, edge = far if isinstance(far, tuple) else (far, None)
    corner = side if corner is None else corner
    return (
        ((off, side), (own, n), (own, 1 - n), (twins[0], inner[0])),
        ((cor, corner), (swap, n), (swap, 1 - n), (twins[1], inner[1])),
        ((far, 2) if edge is None else (edge, corner), (far, n), (far, 1 - n), (twins[2], inner[2])),
    )


def window(table, t, fs, rows=(0, 1, 2)):
    places = [table[row][col + t] for row in rows for col in range(3)]
    return jnp.concatenate([ref[index, :, fs] for ref, index in places], axis=0)


def spread(x):
    lane = lax.broadcasted_iota(jnp.int32, x.shape, 1) // HDIM
    return jnp.concatenate([jnp.where(lane == h, x, jnp.zeros_like(x)) for h in range(GROUP)], axis=0)


def gather_heads(y):
    lane = lax.broadcasted_iota(jnp.int32, (PP, GW), 1) // HDIM
    out = y[0:PP]
    for h in range(1, GROUP):
        out = jnp.where(lane == h, y[h * PP : (h + 1) * PP], out)
    return out


def group_slice(g):
    return pl.ds(pl.multiple_of(g * GW, GW), GW)


def region_flags(here_ref, cloud_ref):
    rows, cols = cloud_ref.shape
    lat, lon = here_ref[0], here_ref[1]
    odd = lon % 2
    sign = 2 * odd - 1
    near = 2 * lon + odd
    outer = jnp.where(lat % 2 == 0, lat - 1, lat + 1)
    within = (outer >= 0) & (outer < rows)
    partner = jnp.where(lat % 2 == 0, lat + 1, lat - 1)
    lines = (lat, partner, jnp.clip(outer, 0, rows - 1))
    inside = (True, True, within)
    clear = []
    for row in range(3):
        line = []
        for col in range(4):
            c = (near + sign * (1 - col) + cols) % cols
            flag = cloud_ref[lines[row], c] == 1
            line.append(flag & within if row == 2 else flag)
        clear.append(line)
    return odd, inside, clear


def segments(flags, fill):
    width = PP * len(flags)
    slot = lax.broadcasted_iota(jnp.int32, (1, width), 1) // PP
    out = jnp.zeros((1, width), F32)
    for i, flag in enumerate(flags):
        if flag is not True:
            value = fill if flag is False else jnp.where(flag, 0.0, fill)
            out = jnp.where(slot == i, value, out)
    return out


def query_flags(clear, t):
    return [
        True if (row, col) == (0, 1) else clear[row][col + t] for row in range(3) for col in range(3)
    ]


def join_kernel(count, *refs):
    out = refs[count]
    at = 0
    for ref in refs[:count]:
        size = ref.shape[0]
        out[at : at + size] = ref[...]
        at += size


def edges_kernel(here_ref, k_ref, v_ref, s_ref, q_ref, cor_ref, qn_ref, off_ref, sems):
    n = here_ref[1] % 2
    copies = [
        pltpu.make_async_copy(ref.at[n], off_ref.at[i], sems.at[i])
        for i, ref in enumerate((k_ref, v_ref, s_ref, q_ref))
    ]
    for c in copies:
        c.start()
    for c in copies:
        c.wait()
    cor_ref[...] = off_ref[0:3]
    qn_ref[0] = off_ref[3]


def faces_kernel(here_ref, *refs):
    n = here_ref[1] % 2
    for i, ref in enumerate(refs[:-1]):
        refs[-1][i] = ref[1 - n]


def grad_pack_kernel(grad_ref, swap_ref, cor_ref, far_ref, face_ref):
    far_ref[0:2] = swap_ref[...]
    far_ref[2] = cor_ref[0]
    face_ref[0] = grad_ref[1]
    face_ref[1] = swap_ref[1]


def key_value_tables(refs, n):
    k, v, k_swap, v_swap, k_far, v_far, cor, edge, off, twin, k_far_twin, v_far_twin = refs
    return (
        region(k, k_swap, (k_far, edge), off, cor, (twin, twin, k_far_twin), n, 0, (0, 4, n)),
        region(v, v_swap, (v_far, edge), off, cor, (twin, twin, v_far_twin), n, 1, (1, 5, n)),
    )


def attend_kernel(here_ref, cloud_ref, q_ref, *rest):
    n, _, clear = region_flags(here_ref, cloud_ref)
    k_table, v_table = key_value_tables(rest[0:12], n)
    att_ref, stat_ref = rest[12:]
    for t in range(2):
        qt = n if t == 0 else 1 - n
        stat_ref[t] = jnp.zeros((PP, 128), F32)
        mask = segments(query_flags(clear, t), NEG_FILL)

        def step(g, carry):
            fs = group_slice(g)
            q = spread(q_ref[qt, :, fs] * SCALE)
            kw = window(k_table, t, fs)
            s = dot(q, kw, NT) + mask
            m = jnp.max(s, axis=1, keepdims=True)
            e = jnp.exp(s - m)
            total = jnp.sum(e, axis=1, keepdims=True)
            p = (e * (1.0 / total)).astype(BF)
            lse = m + jnp.log(total)
            att_ref[t, :, fs] = gather_heads(dot(p, window(v_table, t, fs), NN)).astype(BF)
            lane = lax.broadcasted_iota(jnp.int32, (PP, 128), 1)
            stat = stat_ref[t]
            for h in range(GROUP):
                stat = jnp.where(lane == g * GROUP + h, lse[h * PP : (h + 1) * PP], stat)
            stat_ref[t] = stat
            return carry

        lax.fori_loop(0, GROUPS, step, 0, unroll=True)


def contrast_kernel(here_ref, cloud_ref, att_ref, stat_ref, pair_ref, *rest):
    loss_ref, grad_ref, stats_ref = rest[8:]
    n, _, clear = region_flags(here_ref, cloud_ref)
    s, swap, far, edge, off, cor, twin, far_twin = rest[0:8]
    table = region(s, swap, (far, edge), off, cor, (twin, twin, far_twin), n, side=2, inner=(2, 6, n))
    season = jnp.concatenate([ref[index] for line in table for ref, index in line], axis=0)
    att = jnp.concatenate([att_ref[0], att_ref[1]], axis=0)
    side = lax.broadcasted_iota(jnp.int32, (2 * PP, REG), 0) < PP
    sides = []
    for t in range(2):
        flags = query_flags(clear, t)
        line = []
        for row in range(3):
            mine = flags[row * 3 : row * 3 + 3]
            line += mine + [False] if t == 0 else [False] + mine
        sides.append(segments(line, NEG_FILL))
    mask = jnp.where(side, sides[0], sides[1])
    logits = dot(att, season, NT) + mask
    m = jnp.max(logits, axis=1, keepdims=True)
    e = jnp.exp(logits - m)
    total = jnp.sum(e, axis=1, keepdims=True)
    w = (e * (1.0 / total)).astype(BF)
    ctotal = m + jnp.log(total)
    key = lax.broadcasted_iota(jnp.int32, (4 * PP, PP), 0)
    hits = []
    for t in range(2):
        pair = pair_ref[pl.ds(n if t == 0 else 1 - n, 1), :]
        hits.append((key == pair + (1 + t) * PP).astype(F32))
    hit = jnp.transpose(jnp.concatenate(hits, axis=1)) > 0.5
    chosen = jnp.sum(jnp.where(hit, logits[:, 0 : 4 * PP], 0.0), axis=1, keepdims=True)
    loss = jnp.transpose(jnp.broadcast_to(ctotal - chosen, (2 * PP, 128)))
    for t in range(2):
        loss_ref[pl.ds(n if t == 0 else 1 - n, 1), :] = loss[0:1, t * PP : (t + 1) * PP]
    acc = dot(w, season, NN) - dot(hit.astype(F32).astype(BF), season[0 : 4 * PP], NN)
    grad = acc.astype(BF)
    prod = grad.astype(F32) * att.astype(F32)
    high = prod.astype(BF)
    low = (prod - high.astype(F32)).astype(BF)
    feat = lax.broadcasted_iota(jnp.int32, (WIDTH, 128), 0) // HDIM
    lane = lax.broadcasted_iota(jnp.int32, (WIDTH, 128), 1)
    pick = (lane == feat + HEADS).astype(F32).astype(BF)
    delta = dot(high, pick, NN) + dot(low, pick, NN)
    stat = jnp.concatenate([stat_ref[0], stat_ref[1]], axis=0) + delta
    part0 = stat.astype(BF).astype(F32)
    part1 = (stat - part0).astype(BF).astype(F32)
    part2 = (stat - part0 - part1).astype(BF).astype(F32)
    packed = part0 + pltpu.roll(part1, 32, 1) + pltpu.roll(part2, 64, 1)
    packed = packed.astype(BF)
    for t in range(2):
        rows = slice(t * PP, (t + 1) * PP)
        grad_ref[t, :, 0:WIDTH] = grad[rows]
        grad_ref[t, :, WIDTH:EXT] = packed[rows]
        stats_ref[t] = stat[rows]


def head_column(stat, index):
    lane = lax.broadcasted_iota(jnp.int32, (PP, 128), 1)
    cols = [
        jnp.sum(jnp.where(lane == index + h, stat, 0.0), axis=1, keepdims=True) for h in range(GROUP)
    ]
    return jnp.concatenate(cols, axis=0)


def query_kernel(here_ref, cloud_ref, q_ref, grad_ref, stats_ref, *rest):
    n, _, clear = region_flags(here_ref, cloud_ref)
    k_table, v_table = key_value_tables(rest[0:12], n)
    out_ref = rest[12]
    for t in range(2):
        qt = n if t == 0 else 1 - n
        mask = segments(query_flags(clear, t), NEG_FILL)

        def step(g, carry):
            fs = group_slice(g)
            q = spread(q_ref[qt, :, fs] * SCALE)
            stat = stats_ref[t]
            lse = head_column(stat, g * GROUP)
            delta = head_column(stat, g * GROUP + HEADS)
            kw = window(k_table, t, fs)
            s = dot(q, kw, NT) + mask
            p = jnp.exp(s - lse)
            gd = dot(spread(grad_ref[t, :, fs]), window(v_table, t, fs), NT)
            ds = (p * (gd - delta)).astype(BF)
            out = gather_heads(dot(ds, kw, NN)) * SCALE
            out_ref[qt, :, fs] = out.astype(BF)
            return carry

        lax.fori_loop(0, GROUPS, step, 0, unroll=True)


def key_terms(flags, rows, k_ref, v_ref, n, q_table, g_table, rows_ref, finish):
    inside, clear = flags
    for t in range(2):
        kt = n if t == 0 else 1 - n
        parts = jnp.transpose(window(g_table, t, slice(WIDTH, EXT), rows).astype(F32))
        stats = parts[0:32] + parts[32:64] + parts[64:96]
        seen = clear[0][1 + t]
        open_to = [
            True if (row, col) == (0, 1) else (seen & inside[2] if row == 2 else seen)
            for row in rows
            for col in range(3)
        ]
        rows_ref[0:HEADS] = stats[0:HEADS] + segments(open_to, -NEG_FILL)
        rows_ref[HEADS : 2 * HEADS] = stats[HEADS : 2 * HEADS]

        def step(g, carry):
            fs = group_slice(g)
            ks = spread(k_ref[kt, :, fs] * SCALE)
            vs = spread(v_ref[kt, :, fs])
            qw = window(q_table, t, fs, rows)
            gw = window(g_table, t, fs, rows)
            s = dot(ks, qw, NT)
            gd = dot(vs, gw, NT)
            ps, dss = [], []
            for h in range(GROUP):
                part = slice(h * PP, (h + 1) * PP)
                lse = rows_ref[pl.ds(g * GROUP + h, 1), :]
                delta = rows_ref[pl.ds(HEADS + g * GROUP + h, 1), :]
                p = jnp.exp(s[part] - lse)
                ps.append(p.astype(BF))
                dss.append((p * (gd[part] - delta)).astype(BF))
            p = jnp.concatenate(ps, axis=0)
            ds = jnp.concatenate(dss, axis=0)
            finish(t, kt, fs, gather_heads(dot(ds, qw, NN)), gather_heads(dot(p, gw, NN)))
            return carry

        lax.fori_loop(0, GROUPS, step, 0, unroll=True)


def inner_key_kernel(here_ref, cloud_ref, k_ref, v_ref, *rest):
    q, q_swap, q_off, q_cor, own_twin, q_twin, g, g_swap, g_off, g_cor, g_twin = rest[0:11]
    ksum_ref, vsum_ref, rows_ref = rest[11:]
    n, inside, clear = region_flags(here_ref, cloud_ref)
    q_table = region(q, q_swap, None, q_off, q_cor, (own_twin, q_twin, None), n, side=3, inner=(3, n, None), corner=0)
    g_table = region(g, g_swap, None, g_off, g_cor, (g_twin, g_twin, None), 0, inner=(0, 1, None))

    def finish(t, kt, fs, dk, dv):
        ksum_ref[t, :, fs] = dk
        vsum_ref[t, :, fs] = dv

    key_terms((inside, clear), (0, 1), k_ref, v_ref, n, q_table, g_table, rows_ref, finish)


def outer_key_kernel(here_ref, cloud_ref, k_ref, v_ref, ksum_ref, vsum_ref, *rest):
    q_far, q_twin, g_far, g_twin = rest[0:4]
    kout_ref, vout_ref, rows_ref = rest[4:]
    n, inside, clear = region_flags(here_ref, cloud_ref)
    q_table = region(None, None, q_far, None, None, (None, None, q_twin), n, inner=(n, n, n))
    g_table = region(None, None, g_far, None, None, (None, None, g_twin), 0, inner=(1, 1, 1))

    def finish(t, kt, fs, dk, dv):
        kout_ref[kt, :, fs] = ((ksum_ref[t, :, fs] + dk) * SCALE).astype(BF)
        vout_ref[kt, :, fs] = (vsum_ref[t, :, fs] + dv).astype(BF)

    key_terms((inside, clear), (2,), k_ref, v_ref, n, q_table, g_table, rows_ref, finish)


SMEM = pl.BlockSpec(memory_space=pltpu.SMEM)
VMEM = pl.BlockSpec(memory_space=pltpu.VMEM)
ANY = pl.BlockSpec(memory_space=pl.ANY)


def call(kernel, name, in_specs, out_shape, scratch, flops):
    return pl.pallas_call(
        kernel,
        name=name,
        out_shape=out_shape,
        in_specs=in_specs,
        out_specs=jax.tree.map(lambda _: VMEM, out_shape),
        scratch_shapes=scratch,
        compiler_params=pltpu.CompilerParams(vmem_limit_bytes=VMEM_LIMIT),
        cost_estimate=pl.CostEstimate(flops=flops, bytes_accessed=6_000_000, transcendentals=0),
    )


def shape(dims, dtype):
    return jax.ShapeDtypeStruct(dims, dtype)


def body(way, queries, keys, values, season, cloud, pairing):
    lat = lax.axis_index("lat")
    lon = lax.axis_index("lon")
    q, k, v, s = (x[0] for x in (queries, keys, values, season))

    here = jnp.stack([lat, lon]).astype(jnp.int32)

    def move(x, kind):
        return lax.ppermute(x, AXES, way[kind])

    def named(name, x, kind):
        with jax.named_scope(name + "_" + kind):
            return move(x, kind)

    def joined(*parts):
        total = sum(p.shape[0] for p in parts)
        return call(
            functools.partial(join_kernel, len(parts)),
            "join",
            [VMEM] * len(parts),
            shape((total,) + parts[0].shape[1:], parts[0].dtype),
            [],
            1_000_000,
        )(*parts)

    k_swap = named("key", k, "swap")
    v_swap = named("value", v, "swap")
    cor_near, q_near, nears = call(
        edges_kernel,
        "edges",
        [SMEM] + [ANY] * 4,
        (shape((3, PP, WIDTH), BF), shape((1, PP, WIDTH), BF), shape((4, PP, WIDTH), BF)),
        [pltpu.SemaphoreType.DMA((4,))],
        1_000_000,
    )(here, k, v, s, q)
    k_swap, v_swap, s1, cor_near, nears = phase(k_swap, v_swap, s, cor_near, nears)
    k_far = named("key", k_swap, "far")
    v_far = named("value", v_swap, "far")
    s_swap = named("season", s1, "swap")
    cor = named("kvs", cor_near, "cor")
    off = named("all", nears, "off")
    k_far, v_far, s_swap, cor, off, q1, q_near = phase(k_far, v_far, s_swap, cor, off, q, q_near)
    s_far = named("season", s_swap, "far")
    edge = named("kvs", cor, "far")
    q_swap = named("query", q1, "swap")
    q_cor = named("query", q_near, "cor")
    faces = call(
        faces_kernel,
        "faces",
        [SMEM] + [VMEM] * 7,
        shape((7, PP, WIDTH), BF),
        [],
        1_000_000,
    )(here, k, v, s, q, k_swap, v_swap, s_swap)
    twin = named("inner", faces, "twin")
    s_far, edge, off, twin, q_swap, q_cor = phase(s_far, edge, off, twin, q_swap, q_cor)
    k_far_twin = named("key_far", k_far, "twin")
    v_far_twin = named("value_far", v_far, "twin")
    s_far_twin = named("season_far", s_far, "twin")
    q_far = named("query", joined(q_swap, q_cor), "far")
    kvp = (k, v, k_swap, v_swap, k_far, v_far, cor, edge, off, twin, k_far_twin, v_far_twin)

    att, stat = call(
        attend_kernel,
        "attend",
        [SMEM, SMEM, VMEM] + [VMEM] * 12,
        (shape((2, PP, WIDTH), BF), shape((2, PP, 128), F32)),
        [],
        2_400_000_000,
    )(here, cloud, q, *kvp)

    loss, grad, stats = call(
        contrast_kernel,
        "contrast",
        [SMEM, SMEM, VMEM, VMEM, VMEM] + [VMEM] * 8,
        (shape((2, PP), F32), shape((2, PP, EXT), BF), shape((2, PP, 128), F32)),
        [],
        1_200_000_000,
    )(here, cloud, att, stat, pairing[0], s, s_swap, s_far, edge, off, cor, twin, s_far_twin)

    g_near = grad[0:1]
    g_swap = named("grad", grad, "swap")
    g_cor = named("grad", g_near, "cor")
    g_off = named("grad", g_near, "off")
    query_grad = call(
        query_kernel,
        "query_grads",
        [SMEM, SMEM, VMEM, VMEM, VMEM] + [VMEM] * 12,
        shape((2, PP, WIDTH), BF),
        [],
        3_600_000_000,
    )(here, cloud, q, grad, stats, *kvp)

    g_swap, g_cor, g_off, q_far, query_grad, q_swap1 = phase(
        g_swap, g_cor, g_off, q_far, query_grad, q_swap
    )
    q_swap_twin = named("query", q_swap1, "twin")
    far, faces = call(
        grad_pack_kernel,
        "grad_pack",
        [VMEM] * 3,
        (shape((3, PP, EXT), BF), shape((2, PP, EXT), BF)),
        [],
        1_000_000,
    )(grad, g_swap, g_cor)
    g_far = named("grad", far, "far")
    g_twin = named("grad", faces, "twin")
    q_far_twin = named("query_far", q_far, "twin")

    key_sum, value_sum = call(
        inner_key_kernel,
        "inner_key_grads",
        [SMEM, SMEM, VMEM, VMEM] + [VMEM] * 11,
        (shape((2, PP, WIDTH), F32), shape((2, PP, WIDTH), F32)),
        [pltpu.VMEM((2 * HEADS, 6 * PP), F32)],
        3_200_000_000,
    )(
        here, cloud, k, v, q, q_swap, off, q_cor, twin, q_swap_twin,
        grad, g_swap, g_off, g_cor, g_twin,
    )

    g_far, q_far_twin, key_sum, value_sum = phase(g_far, q_far_twin, key_sum, value_sum)
    g_last = named("grad_last", g_far, "twin")
    key_grad, value_grad = call(
        outer_key_kernel,
        "outer_key_grads",
        [SMEM, SMEM, VMEM, VMEM, VMEM, VMEM] + [VMEM] * 4,
        (shape((2, PP, WIDTH), BF), shape((2, PP, WIDTH), BF)),
        [pltpu.VMEM((2 * HEADS, 3 * PP), F32)],
        1_600_000_000,
    )(here, cloud, k, v, key_sum, value_sum, q_far, q_far_twin, g_far, g_last)

    return (loss[None], query_grad[None], key_grad[None], value_grad[None])


def solution(mesh):
    block = P("lat", "lon", None, None)
    line = P("lat", "lon", None)
    way = routes(mesh.shape["lat"], mesh.shape["lon"])
    return jax.shard_map(
        functools.partial(body, way),
        mesh=mesh,
        in_specs=(block, block, block, block, P(), line),
        out_specs=(line, block, block, block),
        check_vma=False,
    )
```

```python
import functools

import jax
import jax.numpy as jnp
from jax import lax
from jax.experimental import pallas as pl
from jax.experimental.pallas import tpu as pltpu
from jax.sharding import PartitionSpec as P

HEADS = 16
HDIM = 64
PP = 64
WIDTH = HEADS * HDIM
GROUP = 4
GW = GROUP * HDIM
GROUPS = HEADS // GROUP
ROWS = GROUP * PP
WIN = 9 * PP
REG = 12 * PP
EXT = WIDTH + 128
NEG_FILL = -1e30
SCALE = HDIM ** -0.5
AXES = ("lon", "lat")
VMEM_LIMIT = 48 * 1024 * 1024
BF = jnp.bfloat16
F32 = jnp.float32

NT = (((1,), (1,)), ((), ()))
NN = (((1,), (0,)), ((), ()))


def dot(a, b, dims):
    return lax.dot_general(a, b, dims, preferred_element_type=F32)


def routes(rows, cols):
    def at(r, c):
        return (c % cols) * rows + r

    cells = [(r, c) for r in range(rows) for c in range(cols)]

    def away(c):
        return c + 1 if c % 2 else c - 1

    def hop(r):
        return r + 2 if r % 2 == 0 else r - 2

    def past(r):
        return r - 1 if r % 2 == 0 else r + 1

    return dict(
        swap=[(at(r, c), at(r ^ 1, c)) for r, c in cells],
        off=[(at(r, c), at(r, away(c))) for r, c in cells],
        cor=[(at(r, c), at(r ^ 1, away(c))) for r, c in cells],
        far=[(at(r, c), at(hop(r), c)) for r, c in cells if 0 <= hop(r) < rows],
        twin=[(at(r, c), at(r, c ^ 1)) for r, c in cells],
        out=[(at(r, c), at(past(r), c)) for r, c in cells if 0 <= past(r) < rows],
        edge=[(at(r, c), at(past(r), away(c))) for r, c in cells if 0 <= past(r) < rows],
    )


def after(x, *done):
    return lax.optimization_barrier((x,) + done)[0]


def phase(*values):
    return lax.optimization_barrier(values)


def region(own, swap, far, off, cor, twins, n, inner):
    return (
        ((off, 0), (own, n), (own, 1 - n), (twins[0], inner[0])),
        ((cor, 0), (swap, n), (swap, 1 - n), (twins[1], inner[1])),
        ((far, 2), (far, n), (far, 1 - n), (twins[2], inner[2])),
    )


def window(table, t, fs, rows=(0, 1, 2)):
    places = [table[row][col + t] for row in rows for col in range(3)]
    return jnp.concatenate([ref[index, :, fs] for ref, index in places], axis=0)


def spread(x):
    lane = lax.broadcasted_iota(jnp.int32, x.shape, 1) // HDIM
    return jnp.concatenate([jnp.where(lane == h, x, jnp.zeros_like(x)) for h in range(GROUP)], axis=0)


def gather_heads(y):
    lane = lax.broadcasted_iota(jnp.int32, (PP, GW), 1) // HDIM
    out = y[0:PP]
    for h in range(1, GROUP):
        out = jnp.where(lane == h, y[h * PP : (h + 1) * PP], out)
    return out


def group_slice(g):
    return pl.ds(pl.multiple_of(g * GW, GW), GW)


def region_flags(here_ref, cloud_ref):
    rows, cols = cloud_ref.shape
    lat, lon = here_ref[0], here_ref[1]
    odd = lon % 2
    sign = 2 * odd - 1
    near = 2 * lon + odd
    outer = jnp.where(lat % 2 == 0, lat - 1, lat + 1)
    within = (outer >= 0) & (outer < rows)
    partner = jnp.where(lat % 2 == 0, lat + 1, lat - 1)
    lines = (lat, partner, jnp.clip(outer, 0, rows - 1))
    inside = (True, True, within)
    clear = []
    for row in range(3):
        line = []
        for col in range(4):
            c = (near + sign * (1 - col) + cols) % cols
            flag = cloud_ref[lines[row], c] == 1
            line.append(flag & within if row == 2 else flag)
        clear.append(line)
    return odd, inside, clear


def segments(flags, fill):
    width = PP * len(flags)
    slot = lax.broadcasted_iota(jnp.int32, (1, width), 1) // PP
    out = jnp.zeros((1, width), F32)
    for i, flag in enumerate(flags):
        if flag is not True:
            value = fill if flag is False else jnp.where(flag, 0.0, fill)
            out = jnp.where(slot == i, value, out)
    return out


def query_flags(clear, t):
    return [
        True if (row, col) == (0, 1) else clear[row][col + t] for row in range(3) for col in range(3)
    ]


def join_kernel(count, *refs):
    out = refs[count]
    at = 0
    for ref in refs[:count]:
        size = ref.shape[0]
        out[at : at + size] = ref[...]
        at += size


def edges_kernel(here_ref, pair_ref, k_ref, v_ref, s_ref, q_ref, off_ref, qn_ref, pair_out, sems):
    n = here_ref[1] % 2
    copies = [
        pltpu.make_async_copy(
            ref.at[n], off_ref.at[i] if i < 3 else qn_ref.at[0], sems.at[i]
        )
        for i, ref in enumerate((k_ref, v_ref, s_ref, q_ref))
    ]
    for c in copies:
        c.start()
    pair_out[...] = pair_ref[...]
    for c in copies:
        c.wait()


def pack_kernel(here_ref, k_ref, v_ref, s_ref, q_ref, ks_ref, vs_ref, ss_ref, kf_ref, vf_ref, cor_ref,
                far_ref, face_ref):
    n = here_ref[1] % 2
    far_ref[0:2] = ss_ref[...]
    far_ref[2:5] = cor_ref[...]
    for i, ref in enumerate((k_ref, v_ref, s_ref, q_ref, ks_ref, vs_ref, ss_ref, kf_ref, vf_ref)):
        face_ref[i] = ref[1 - n]


def grad_pack_kernel(grad_ref, swap_ref, cor_ref, far_ref, face_ref):
    far_ref[0:2] = swap_ref[...]
    far_ref[2] = cor_ref[0]
    face_ref[0] = grad_ref[1]
    face_ref[1] = swap_ref[1]


def key_value_tables(refs, n):
    k, v, k_swap, v_swap, k_far, v_far, far, cor, off, twin = refs
    return [
        (
            ((off, i), (own, n), (own, 1 - n), (twin, i)),
            ((cor, i), (swap, n), (swap, 1 - n), (twin, 4 + i)),
            ((far, 2 + i), (outer, n), (outer, 1 - n), (twin, 7 + i)),
        )
        for i, (own, swap, outer) in enumerate(((k, k_swap, k_far), (v, v_swap, v_far)))
    ]


def attend_kernel(here_ref, cloud_ref, q_ref, *rest):
    n, _, clear = region_flags(here_ref, cloud_ref)
    k_table, v_table = key_value_tables(rest[0:10], n)
    att_ref, stat_ref = rest[10:]
    for t in range(2):
        qt = n if t == 0 else 1 - n
        stat_ref[t] = jnp.zeros((PP, 128), F32)
        mask = segments(query_flags(clear, t), NEG_FILL)

        def step(g, carry):
            fs = group_slice(g)
            q = spread(q_ref[qt, :, fs] * SCALE)
            kw = window(k_table, t, fs)
            s = dot(q, kw, NT) + mask
            m = jnp.max(s, axis=1, keepdims=True)
            e = jnp.exp(s - m)
            total = jnp.sum(e, axis=1, keepdims=True)
            p = (e * (1.0 / total)).astype(BF)
            lse = m + jnp.log(total)
            att_ref[t, :, fs] = gather_heads(dot(p, window(v_table, t, fs), NN)).astype(BF)
            lane = lax.broadcasted_iota(jnp.int32, (PP, 128), 1)
            stat = stat_ref[t]
            for h in range(GROUP):
                stat = jnp.where(lane == g * GROUP + h, lse[h * PP : (h + 1) * PP], stat)
            stat_ref[t] = stat
            return carry

        lax.fori_loop(0, GROUPS, step, 0, unroll=True)


def contrast_kernel(here_ref, cloud_ref, att_ref, stat_ref, pair_ref, *rest):
    loss_ref, grad_ref, stats_ref = rest[7:]
    n, _, clear = region_flags(here_ref, cloud_ref)
    s, swap, far, off, cor, twin, far_twin = rest[0:7]
    table = (
        ((off, 2), (s, n), (s, 1 - n), (twin, 2)),
        ((cor, 2), (swap, n), (swap, 1 - n), (twin, 6)),
        ((far, 4), (far, n), (far, 1 - n), (far_twin, n)),
    )
    season = jnp.concatenate([ref[index] for line in table for ref, index in line], axis=0)
    att = jnp.concatenate([att_ref[0], att_ref[1]], axis=0)
    side = lax.broadcasted_iota(jnp.int32, (2 * PP, REG), 0) < PP
    sides = []
    for t in range(2):
        flags = query_flags(clear, t)
        line = []
        for row in range(3):
            mine = flags[row * 3 : row * 3 + 3]
            line += mine + [False] if t == 0 else [False] + mine
        sides.append(segments(line, NEG_FILL))
    mask = jnp.where(side, sides[0], sides[1])
    logits = dot(att, season, NT) + mask
    m = jnp.max(logits, axis=1, keepdims=True)
    e = jnp.exp(logits - m)
    total = jnp.sum(e, axis=1, keepdims=True)
    w = (e * (1.0 / total)).astype(BF)
    ctotal = m + jnp.log(total)
    key = lax.broadcasted_iota(jnp.int32, (4 * PP, PP), 0)
    hits = []
    for t in range(2):
        pair = pair_ref[pl.ds(n if t == 0 else 1 - n, 1), :]
        hits.append((key == pair + (1 + t) * PP).astype(F32))
    hit = jnp.transpose(jnp.concatenate(hits, axis=1)) > 0.5
    chosen = jnp.sum(jnp.where(hit, logits[:, 0 : 4 * PP], 0.0), axis=1, keepdims=True)
    loss = jnp.transpose(jnp.broadcast_to(ctotal - chosen, (2 * PP, 128)))
    for t in range(2):
        loss_ref[pl.ds(n if t == 0 else 1 - n, 1), :] = loss[0:1, t * PP : (t + 1) * PP]
    acc = dot(w, season, NN) - dot(hit.astype(F32).astype(BF), season[0 : 4 * PP], NN)
    grad = acc.astype(BF)
    prod = grad.astype(F32) * att.astype(F32)
    high = prod.astype(BF)
    low = (prod - high.astype(F32)).astype(BF)
    feat = lax.broadcasted_iota(jnp.int32, (WIDTH, 128), 0) // HDIM
    lane = lax.broadcasted_iota(jnp.int32, (WIDTH, 128), 1)
    pick = (lane == feat + HEADS).astype(F32).astype(BF)
    delta = dot(high, pick, NN) + dot(low, pick, NN)
    stat = jnp.concatenate([stat_ref[0], stat_ref[1]], axis=0) + delta
    part0 = stat.astype(BF).astype(F32)
    part1 = (stat - part0).astype(BF).astype(F32)
    part2 = (stat - part0 - part1).astype(BF).astype(F32)
    packed = part0 + pltpu.roll(part1, 32, 1) + pltpu.roll(part2, 64, 1)
    packed = packed.astype(BF)
    for t in range(2):
        rows = slice(t * PP, (t + 1) * PP)
        grad_ref[t, :, 0:WIDTH] = grad[rows]
        grad_ref[t, :, WIDTH:EXT] = packed[rows]
        stats_ref[t] = stat[rows]


def head_column(stat, index):
    lane = lax.broadcasted_iota(jnp.int32, (PP, 128), 1)
    cols = [
        jnp.sum(jnp.where(lane == index + h, stat, 0.0), axis=1, keepdims=True) for h in range(GROUP)
    ]
    return jnp.concatenate(cols, axis=0)


def query_kernel(here_ref, cloud_ref, q_ref, grad_ref, stats_ref, *rest):
    n, _, clear = region_flags(here_ref, cloud_ref)
    k_table, v_table = key_value_tables(rest[0:10], n)
    out_ref = rest[10]
    for t in range(2):
        qt = n if t == 0 else 1 - n
        mask = segments(query_flags(clear, t), NEG_FILL)

        def step(g, carry):
            fs = group_slice(g)
            q = spread(q_ref[qt, :, fs] * SCALE)
            stat = stats_ref[t]
            lse = head_column(stat, g * GROUP)
            delta = head_column(stat, g * GROUP + HEADS)
            kw = window(k_table, t, fs)
            s = dot(q, kw, NT) + mask
            p = jnp.exp(s - lse)
            gd = dot(spread(grad_ref[t, :, fs]), window(v_table, t, fs), NT)
            ds = (p * (gd - delta)).astype(BF)
            out = gather_heads(dot(ds, kw, NN)) * SCALE
            out_ref[qt, :, fs] = out.astype(BF)
            return carry

        lax.fori_loop(0, GROUPS, step, 0, unroll=True)


def key_terms(flags, rows, k_ref, v_ref, n, q_table, g_table, rows_ref, finish, blocks=(0, 1)):
    inside, clear = flags
    for t in blocks:
        kt = n if t == 0 else 1 - n
        parts = jnp.transpose(window(g_table, t, slice(WIDTH, EXT), rows).astype(F32))
        stats = parts[0:32] + parts[32:64] + parts[64:96]
        seen = clear[0][1 + t]
        open_to = [
            True if (row, col) == (0, 1) else (seen & inside[2] if row == 2 else seen)
            for row in rows
            for col in range(3)
        ]
        rows_ref[0:HEADS] = stats[0:HEADS] + segments(open_to, -NEG_FILL)
        rows_ref[HEADS : 2 * HEADS] = stats[HEADS : 2 * HEADS]

        def step(g, carry):
            fs = group_slice(g)
            ks = spread(k_ref[kt, :, fs] * SCALE)
            vs = spread(v_ref[kt, :, fs])
            qw = window(q_table, t, fs, rows)
            gw = window(g_table, t, fs, rows)
            s = dot(ks, qw, NT)
            gd = dot(vs, gw, NT)
            ps, dss = [], []
            for h in range(GROUP):
                part = slice(h * PP, (h + 1) * PP)
                lse = rows_ref[pl.ds(g * GROUP + h, 1), :]
                delta = rows_ref[pl.ds(HEADS + g * GROUP + h, 1), :]
                p = jnp.exp(s[part] - lse)
                ps.append(p.astype(BF))
                dss.append((p * (gd[part] - delta)).astype(BF))
            p = jnp.concatenate(ps, axis=0)
            ds = jnp.concatenate(dss, axis=0)
            finish(t, kt, fs, gather_heads(dot(ds, qw, NN)), gather_heads(dot(p, gw, NN)))
            return carry

        lax.fori_loop(0, GROUPS, step, 0, unroll=True)


def inner_key_kernel(here_ref, cloud_ref, k_ref, v_ref, *rest):
    q, q_swap, q_off, q_cor, own_twin, q_twin, g, g_swap, g_off, g_cor, g_twin = rest[0:11]
    ksum_ref, vsum_ref, rows_ref = rest[11:]
    n, inside, clear = region_flags(here_ref, cloud_ref)
    q_table = region(q, q_swap, None, q_off, q_cor, (own_twin, q_twin, None), n, (3, n, None))
    g_table = region(g, g_swap, None, g_off, g_cor, (g_twin, g_twin, None), 0, (0, 1, None))

    def finish(t, kt, fs, dk, dv):
        ksum_ref[t, :, fs] = dk
        vsum_ref[t, :, fs] = dv

    key_terms((inside, clear), (0, 1), k_ref, v_ref, n, q_table, g_table, rows_ref, finish)


def outer_near_kernel(here_ref, cloud_ref, k_ref, v_ref, ksum_ref, vsum_ref, *rest):
    q_far, g_far, kout_ref, vout_ref, rows_ref = rest
    n, inside, clear = region_flags(here_ref, cloud_ref)
    q_table = region(None, None, q_far, None, None, (None,) * 3, n, (None,) * 3)
    g_table = region(None, None, g_far, None, None, (None,) * 3, 0, (None,) * 3)

    def finish(t, kt, fs, dk, dv):
        kout_ref[:, fs] = ((ksum_ref[t, :, fs] + dk) * SCALE).astype(BF)
        vout_ref[:, fs] = (vsum_ref[t, :, fs] + dv).astype(BF)

    key_terms((inside, clear), (2,), k_ref, v_ref, n, q_table, g_table, rows_ref, finish, (0,))


def outer_face_kernel(here_ref, cloud_ref, k_ref, v_ref, ksum_ref, vsum_ref, *rest):
    q_far, q_twin, g_far, g_twin, k_near_ref, v_near_ref, kout_ref, vout_ref, rows_ref = rest
    n, inside, clear = region_flags(here_ref, cloud_ref)
    kout_ref[n] = k_near_ref[...]
    vout_ref[n] = v_near_ref[...]
    q_table = region(None, None, q_far, None, None, (None, None, q_twin), n, (n, n, n))
    g_table = region(None, None, g_far, None, None, (None, None, g_twin), 0, (1, 1, 1))

    def finish(t, kt, fs, dk, dv):
        kout_ref[kt, :, fs] = ((ksum_ref[t, :, fs] + dk) * SCALE).astype(BF)
        vout_ref[kt, :, fs] = (vsum_ref[t, :, fs] + dv).astype(BF)

    key_terms((inside, clear), (2,), k_ref, v_ref, n, q_table, g_table, rows_ref, finish, (1,))


SMEM = pl.BlockSpec(memory_space=pltpu.SMEM)
VMEM = pl.BlockSpec(memory_space=pltpu.VMEM)
ANY = pl.BlockSpec(memory_space=pl.ANY)


def call(kernel, name, in_specs, out_shape, scratch):
    return pl.pallas_call(
        kernel,
        name=name,
        out_shape=out_shape,
        in_specs=in_specs,
        out_specs=jax.tree.map(lambda _: VMEM, out_shape),
        scratch_shapes=scratch,
        compiler_params=pltpu.CompilerParams(vmem_limit_bytes=VMEM_LIMIT),
        cost_estimate=pl.CostEstimate(flops=1000, bytes_accessed=1000, transcendentals=0),
    )


def shape(dims, dtype):
    return jax.ShapeDtypeStruct(dims, dtype)


def body(way, queries, keys, values, season, cloud, pairing):
    lat = lax.axis_index("lat")
    lon = lax.axis_index("lon")
    q, k, v, s = (x[0] for x in (queries, keys, values, season))

    here = jnp.stack([lat, lon]).astype(jnp.int32)

    def move(x, kind):
        return lax.ppermute(x, AXES, way[kind])

    def named(name, x, kind):
        with jax.named_scope(name + "_" + kind):
            return move(x, kind)

    def joined(*parts):
        total = sum(p.shape[0] for p in parts)
        return call(
            functools.partial(join_kernel, len(parts)),
            "join",
            [VMEM] * len(parts),
            shape((total,) + parts[0].shape[1:], parts[0].dtype),
            [],
        )(*parts)

    k_swap = named("key", k, "swap")
    v_swap = named("value", v, "swap")
    edge, q_near, pair = call(
        edges_kernel,
        "edges",
        [SMEM, VMEM] + [ANY] * 4,
        (
            shape((3, PP, WIDTH), BF),
            shape((1, PP, WIDTH), BF),
            shape((2, PP), jnp.int32),
        ),
        [pltpu.SemaphoreType.DMA((4,))],
    )(here, pairing[0], k, v, s, q)
    k_swap, v_swap, s1, edge = phase(k_swap, v_swap, s, edge)
    cor = named("kvs", edge, "cor")
    k_far = named("key", k_swap, "far")
    v_far = named("value", v_swap, "far")
    s_swap = named("season", s1, "swap")
    k_far, v_far, cor, s_swap, edge, q1, q_near = phase(k_far, v_far, cor, s_swap, edge, q, q_near)
    far_stack, faces = call(
        pack_kernel,
        "pack",
        [SMEM] + [VMEM] * 10,
        (shape((5, PP, WIDTH), BF), shape((9, PP, WIDTH), BF)),
        [],
    )(here, k, v, s, q, k_swap, v_swap, s_swap, k_far, v_far, cor)
    far = named("season", far_stack, "far")
    off = named("kvs", edge, "off")
    q_swap = named("query", q1, "swap")
    q_cor = named("query", q_near, "cor")
    twin = named("faces", faces, "twin")
    twin, q_cor, off, q_swap, far = phase(twin, q_cor, off, q_swap, far)
    far_twin = named("season_far", far, "twin")
    q_far = named("query", joined(q_swap, q_cor), "far")
    kvp = (k, v, k_swap, v_swap, k_far, v_far, far, cor, off, twin)

    att, stat = call(
        attend_kernel,
        "attend",
        [SMEM, SMEM, VMEM] + [VMEM] * 10,
        (shape((2, PP, WIDTH), BF), shape((2, PP, 128), F32)),
        [],
    )(here, cloud, q, *kvp)

    loss, grad, stats = call(
        contrast_kernel,
        "contrast",
        [SMEM, SMEM, VMEM, VMEM, VMEM] + [VMEM] * 7,
        (shape((2, PP), F32), shape((2, PP, EXT), BF), shape((2, PP, 128), F32)),
        [],
    )(here, cloud, att, stat, pair, s, s_swap, far, off, cor, twin, far_twin)

    g_near = grad[0:1]
    g_swap = named("grad", grad, "swap")
    g_cor = named("grad", g_near, "cor")
    g_off = named("grad", g_near, "off")
    query_grad = call(
        query_kernel,
        "query_grads",
        [SMEM, SMEM, VMEM, VMEM, VMEM] + [VMEM] * 10,
        shape((2, PP, WIDTH), BF),
        [],
    )(here, cloud, q, grad, stats, *kvp)

    q_off = named("query", after(q_near, grad), "off")
    g_swap, g_cor, g_off, q_off, q_far, query_grad, q_swap1 = phase(
        g_swap, g_cor, g_off, q_off, q_far, query_grad, q_swap
    )
    q_swap_twin = named("query", q_swap1, "twin")
    far_stack, faces = call(
        grad_pack_kernel,
        "grad_pack",
        [VMEM] * 3,
        (shape((3, PP, EXT), BF), shape((2, PP, EXT), BF)),
        [],
    )(grad, g_swap, g_cor)
    g_far = named("grad", far_stack, "far")
    g_twin = named("grad", faces, "twin")
    q_far_twin = named("query_far", q_far, "twin")

    key_sum, value_sum = call(
        inner_key_kernel,
        "inner_key_grads",
        [SMEM, SMEM, VMEM, VMEM] + [VMEM] * 11,
        (shape((2, PP, WIDTH), F32), shape((2, PP, WIDTH), F32)),
        [pltpu.VMEM((2 * HEADS, 6 * PP), F32)],
    )(
        here, cloud, k, v, q, q_swap, q_off, q_cor, twin, q_swap_twin,
        grad, g_swap, g_off, g_cor, g_twin,
    )

    g_far, q_far_twin, key_sum, value_sum = phase(g_far, q_far_twin, key_sum, value_sum)
    g_last = named("grad_last", g_far, "twin")
    k_near_grad, v_near_grad = call(
        outer_near_kernel,
        "outer_near_key_grads",
        [SMEM, SMEM] + [VMEM] * 6,
        (shape((PP, WIDTH), BF), shape((PP, WIDTH), BF)),
        [pltpu.VMEM((2 * HEADS, 3 * PP), F32)],
    )(here, cloud, k, v, key_sum, value_sum, q_far, g_far)
    key_grad, value_grad = call(
        outer_face_kernel,
        "outer_face_key_grads",
        [SMEM, SMEM] + [VMEM] * 10,
        (shape((2, PP, WIDTH), BF), shape((2, PP, WIDTH), BF)),
        [pltpu.VMEM((2 * HEADS, 3 * PP), F32)],
    )(
        here, cloud, k, v, key_sum, value_sum, q_far, q_far_twin, g_far, g_last,
        k_near_grad, v_near_grad,
    )

    return (loss[None], query_grad[None], key_grad[None], value_grad[None])


def solution(mesh):
    block = P("lat", "lon", None, None)
    line = P("lat", "lon", None)
    way = routes(mesh.shape["lat"], mesh.shape["lon"])
    return jax.shard_map(
        functools.partial(body, way),
        mesh=mesh,
        in_specs=(block, block, block, block, P(), line),
        out_specs=(line, block, block, block),
        check_vma=False,
    )
```

```python
import functools

import jax
import jax.numpy as jnp
from jax import lax
from jax.experimental import pallas as pl
from jax.experimental.pallas import tpu as pltpu
from jax.sharding import PartitionSpec as P

HEADS = 16
HDIM = 64
PP = 64
WIDTH = HEADS * HDIM
GROUP = 4
GW = GROUP * HDIM
GROUPS = HEADS // GROUP
ROWS = GROUP * PP
WIN = 9 * PP
REG = 12 * PP
EXT = WIDTH + 128
NEG_FILL = -1e30
SCALE = HDIM ** -0.5
AXES = ("lon", "lat")
VMEM_LIMIT = 48 * 1024 * 1024
BF = jnp.bfloat16
F32 = jnp.float32

NT = (((1,), (1,)), ((), ()))
NN = (((1,), (0,)), ((), ()))


def dot(a, b, dims):
    return lax.dot_general(a, b, dims, preferred_element_type=F32)


def routes(rows, cols):
    def at(r, c):
        return (c % cols) * rows + r

    cells = [(r, c) for r in range(rows) for c in range(cols)]

    def away(c):
        return c + 1 if c % 2 else c - 1

    def hop(r):
        return r + 2 if r % 2 == 0 else r - 2

    def past(r):
        return r - 1 if r % 2 == 0 else r + 1

    return dict(
        swap=[(at(r, c), at(r ^ 1, c)) for r, c in cells],
        off=[(at(r, c), at(r, away(c))) for r, c in cells],
        cor=[(at(r, c), at(r ^ 1, away(c))) for r, c in cells],
        far=[(at(r, c), at(hop(r), c)) for r, c in cells if 0 <= hop(r) < rows],
        twin=[(at(r, c), at(r, c ^ 1)) for r, c in cells],
        out=[(at(r, c), at(past(r), c)) for r, c in cells if 0 <= past(r) < rows],
        edge=[(at(r, c), at(past(r), away(c))) for r, c in cells if 0 <= past(r) < rows],
    )


def after(x, *done):
    return lax.optimization_barrier((x,) + done)[0]


def phase(*values):
    return lax.optimization_barrier(values)


def region(own, swap, far, off, cor, twins, n, inner):
    return (
        ((off, 0), (own, n), (own, 1 - n), (twins[0], inner[0])),
        ((cor, 0), (swap, n), (swap, 1 - n), (twins[1], inner[1])),
        ((far, 2), (far, n), (far, 1 - n), (twins[2], inner[2])),
    )


def window(table, t, fs, rows=(0, 1, 2)):
    places = [table[row][col + t] for row in rows for col in range(3)]
    return jnp.concatenate([ref[index, :, fs] for ref, index in places], axis=0)


def spread(x):
    lane = lax.broadcasted_iota(jnp.int32, x.shape, 1) // HDIM
    return jnp.concatenate([jnp.where(lane == h, x, jnp.zeros_like(x)) for h in range(GROUP)], axis=0)


def gather_heads(y):
    lane = lax.broadcasted_iota(jnp.int32, (PP, GW), 1) // HDIM
    out = y[0:PP]
    for h in range(1, GROUP):
        out = jnp.where(lane == h, y[h * PP : (h + 1) * PP], out)
    return out


def group_slice(g):
    return pl.ds(pl.multiple_of(g * GW, GW), GW)


def region_flags(here_ref, cloud_ref):
    rows, cols = cloud_ref.shape
    lat, lon = here_ref[0], here_ref[1]
    odd = lon % 2
    sign = 2 * odd - 1
    near = 2 * lon + odd
    outer = jnp.where(lat % 2 == 0, lat - 1, lat + 1)
    within = (outer >= 0) & (outer < rows)
    partner = jnp.where(lat % 2 == 0, lat + 1, lat - 1)
    lines = (lat, partner, jnp.clip(outer, 0, rows - 1))
    inside = (True, True, within)
    clear = []
    for row in range(3):
        line = []
        for col in range(4):
            c = (near + sign * (1 - col) + cols) % cols
            flag = cloud_ref[lines[row], c] == 1
            line.append(flag & within if row == 2 else flag)
        clear.append(line)
    return odd, inside, clear


def segments(flags, fill):
    width = PP * len(flags)
    slot = lax.broadcasted_iota(jnp.int32, (1, width), 1) // PP
    out = jnp.zeros((1, width), F32)
    for i, flag in enumerate(flags):
        if flag is not True:
            value = fill if flag is False else jnp.where(flag, 0.0, fill)
            out = jnp.where(slot == i, value, out)
    return out


def query_flags(clear, t):
    return [
        True if (row, col) == (0, 1) else clear[row][col + t] for row in range(3) for col in range(3)
    ]


def join_kernel(count, *refs):
    out = refs[count]
    at = 0
    for ref in refs[:count]:
        size = ref.shape[0]
        out[at : at + size] = ref[...]
        at += size


def edges_kernel(here_ref, pair_ref, k_ref, v_ref, s_ref, q_ref, off_ref, qn_ref, pair_out, sems):
    n = here_ref[1] % 2
    copies = [
        pltpu.make_async_copy(
            ref.at[n], off_ref.at[i] if i < 3 else qn_ref.at[0], sems.at[i]
        )
        for i, ref in enumerate((k_ref, v_ref, s_ref, q_ref))
    ]
    for c in copies:
        c.start()
    pair_out[...] = pair_ref[...]
    for c in copies:
        c.wait()


def pack_kernel(here_ref, k_ref, v_ref, s_ref, q_ref, ks_ref, vs_ref, ss_ref, kf_ref, vf_ref, cor_ref,
                far_ref, face_ref):
    n = here_ref[1] % 2
    far_ref[0:2] = ss_ref[...]
    far_ref[2:5] = cor_ref[...]
    for i, ref in enumerate((k_ref, v_ref, s_ref, q_ref, ks_ref, vs_ref, ss_ref, kf_ref, vf_ref)):
        face_ref[i] = ref[1 - n]


def grad_pack_kernel(grad_ref, swap_ref, cor_ref, far_ref, face_ref):
    far_ref[0:2] = swap_ref[...]
    far_ref[2] = cor_ref[0]
    face_ref[0] = grad_ref[1]
    face_ref[1] = swap_ref[1]


def key_value_tables(refs, n):
    k, v, k_swap, v_swap, k_far, v_far, far, cor, off, twin = refs
    return [
        (
            ((off, i), (own, n), (own, 1 - n), (twin, i)),
            ((cor, i), (swap, n), (swap, 1 - n), (twin, 4 + i)),
            ((far, 2 + i), (outer, n), (outer, 1 - n), (twin, 7 + i)),
        )
        for i, (own, swap, outer) in enumerate(((k, k_swap, k_far), (v, v_swap, v_far)))
    ]


def attend_kernel(here_ref, cloud_ref, q_ref, *rest):
    n, _, clear = region_flags(here_ref, cloud_ref)
    k_table, v_table = key_value_tables(rest[0:10], n)
    att_ref, stat_ref = rest[10:]
    for t in range(2):
        qt = n if t == 0 else 1 - n
        stat_ref[t] = jnp.zeros((PP, 128), F32)
        mask = segments(query_flags(clear, t), NEG_FILL)

        def step(g, carry):
            fs = group_slice(g)
            q = spread(q_ref[qt, :, fs] * SCALE)
            kw = window(k_table, t, fs)
            s = dot(q, kw, NT) + mask
            m = jnp.max(s, axis=1, keepdims=True)
            e = jnp.exp(s - m)
            total = jnp.sum(e, axis=1, keepdims=True)
            p = (e * (1.0 / total)).astype(BF)
            lse = m + jnp.log(total)
            att_ref[t, :, fs] = gather_heads(dot(p, window(v_table, t, fs), NN)).astype(BF)
            lane = lax.broadcasted_iota(jnp.int32, (PP, 128), 1)
            stat = stat_ref[t]
            for h in range(GROUP):
                stat = jnp.where(lane == g * GROUP + h, lse[h * PP : (h + 1) * PP], stat)
            stat_ref[t] = stat
            return carry

        lax.fori_loop(0, GROUPS, step, 0, unroll=True)


def contrast_kernel(here_ref, cloud_ref, att_ref, stat_ref, pair_ref, *rest):
    loss_ref, grad_ref, stats_ref = rest[7:]
    n, _, clear = region_flags(here_ref, cloud_ref)
    s, swap, far, off, cor, twin, far_twin = rest[0:7]
    table = (
        ((off, 2), (s, n), (s, 1 - n), (twin, 2)),
        ((cor, 2), (swap, n), (swap, 1 - n), (twin, 6)),
        ((far, 4), (far, n), (far, 1 - n), (far_twin, n)),
    )
    season = jnp.concatenate([ref[index] for line in table for ref, index in line], axis=0)
    att = jnp.concatenate([att_ref[0], att_ref[1]], axis=0)
    side = lax.broadcasted_iota(jnp.int32, (2 * PP, REG), 0) < PP
    sides = []
    for t in range(2):
        flags = query_flags(clear, t)
        line = []
        for row in range(3):
            mine = flags[row * 3 : row * 3 + 3]
            line += mine + [False] if t == 0 else [False] + mine
        sides.append(segments(line, NEG_FILL))
    mask = jnp.where(side, sides[0], sides[1])
    logits = dot(att, season, NT) + mask
    m = jnp.max(logits, axis=1, keepdims=True)
    e = jnp.exp(logits - m)
    total = jnp.sum(e, axis=1, keepdims=True)
    w = (e * (1.0 / total)).astype(BF)
    ctotal = m + jnp.log(total)
    key = lax.broadcasted_iota(jnp.int32, (4 * PP, PP), 0)
    hits = []
    for t in range(2):
        pair = pair_ref[pl.ds(n if t == 0 else 1 - n, 1), :]
        hits.append((key == pair + (1 + t) * PP).astype(F32))
    hit = jnp.transpose(jnp.concatenate(hits, axis=1)) > 0.5
    chosen = jnp.sum(jnp.where(hit, logits[:, 0 : 4 * PP], 0.0), axis=1, keepdims=True)
    loss = jnp.transpose(jnp.broadcast_to(ctotal - chosen, (2 * PP, 128)))
    for t in range(2):
        loss_ref[pl.ds(n if t == 0 else 1 - n, 1), :] = loss[0:1, t * PP : (t + 1) * PP]
    acc = dot(w, season, NN) - dot(hit.astype(F32).astype(BF), season[0 : 4 * PP], NN)
    grad = acc.astype(BF)
    prod = grad.astype(F32) * att.astype(F32)
    high = prod.astype(BF)
    low = (prod - high.astype(F32)).astype(BF)
    feat = lax.broadcasted_iota(jnp.int32, (WIDTH, 128), 0) // HDIM
    lane = lax.broadcasted_iota(jnp.int32, (WIDTH, 128), 1)
    pick = (lane == feat + HEADS).astype(F32).astype(BF)
    delta = dot(high, pick, NN) + dot(low, pick, NN)
    stat = jnp.concatenate([stat_ref[0], stat_ref[1]], axis=0) + delta
    part0 = stat.astype(BF).astype(F32)
    part1 = (stat - part0).astype(BF).astype(F32)
    part2 = (stat - part0 - part1).astype(BF).astype(F32)
    packed = part0 + pltpu.roll(part1, 32, 1) + pltpu.roll(part2, 64, 1)
    packed = packed.astype(BF)
    for t in range(2):
        rows = slice(t * PP, (t + 1) * PP)
        grad_ref[t, :, 0:WIDTH] = grad[rows]
        grad_ref[t, :, WIDTH:EXT] = packed[rows]
        stats_ref[t] = stat[rows]


def head_column(stat, index):
    lane = lax.broadcasted_iota(jnp.int32, (PP, 128), 1)
    cols = [
        jnp.sum(jnp.where(lane == index + h, stat, 0.0), axis=1, keepdims=True) for h in range(GROUP)
    ]
    return jnp.concatenate(cols, axis=0)


def query_kernel(here_ref, cloud_ref, q_ref, grad_ref, stats_ref, *rest):
    n, _, clear = region_flags(here_ref, cloud_ref)
    k_table, v_table = key_value_tables(rest[0:10], n)
    out_ref = rest[10]
    for t in range(2):
        qt = n if t == 0 else 1 - n
        mask = segments(query_flags(clear, t), NEG_FILL)

        def step(g, carry):
            fs = group_slice(g)
            q = spread(q_ref[qt, :, fs] * SCALE)
            stat = stats_ref[t]
            lse = head_column(stat, g * GROUP)
            delta = head_column(stat, g * GROUP + HEADS)
            kw = window(k_table, t, fs)
            s = dot(q, kw, NT) + mask
            p = jnp.exp(s - lse)
            gd = dot(spread(grad_ref[t, :, fs]), window(v_table, t, fs), NT)
            ds = (p * (gd - delta)).astype(BF)
            out = gather_heads(dot(ds, kw, NN)) * SCALE
            out_ref[qt, :, fs] = out.astype(BF)
            return carry

        lax.fori_loop(0, GROUPS, step, 0, unroll=True)


def key_terms(flags, rows, k_ref, v_ref, n, q_table, g_table, rows_ref, finish, blocks=(0, 1)):
    inside, clear = flags
    for t in blocks:
        kt = n if t == 0 else 1 - n
        parts = jnp.transpose(window(g_table, t, slice(WIDTH, EXT), rows).astype(F32))
        stats = parts[0:32] + parts[32:64] + parts[64:96]
        seen = clear[0][1 + t]
        open_to = [
            True if (row, col) == (0, 1) else (seen & inside[2] if row == 2 else seen)
            for row in rows
            for col in range(3)
        ]
        rows_ref[0:HEADS] = stats[0:HEADS] + segments(open_to, -NEG_FILL)
        rows_ref[HEADS : 2 * HEADS] = stats[HEADS : 2 * HEADS]

        def step(g, carry):
            fs = group_slice(g)
            ks = spread(k_ref[kt, :, fs] * SCALE)
            vs = spread(v_ref[kt, :, fs])
            qw = window(q_table, t, fs, rows)
            gw = window(g_table, t, fs, rows)
            s = dot(ks, qw, NT)
            gd = dot(vs, gw, NT)
            ps, dss = [], []
            for h in range(GROUP):
                part = slice(h * PP, (h + 1) * PP)
                lse = rows_ref[pl.ds(g * GROUP + h, 1), :]
                delta = rows_ref[pl.ds(HEADS + g * GROUP + h, 1), :]
                p = jnp.exp(s[part] - lse)
                ps.append(p.astype(BF))
                dss.append((p * (gd[part] - delta)).astype(BF))
            p = jnp.concatenate(ps, axis=0)
            ds = jnp.concatenate(dss, axis=0)
            finish(t, kt, fs, gather_heads(dot(ds, qw, NN)), gather_heads(dot(p, gw, NN)))
            return carry

        lax.fori_loop(0, GROUPS, step, 0, unroll=True)


def inner_key_kernel(here_ref, cloud_ref, k_ref, v_ref, *rest):
    q, q_swap, q_off, q_cor, own_twin, q_twin, g, g_swap, g_off, g_cor, g_twin = rest[0:11]
    ksum_ref, vsum_ref, rows_ref = rest[11:]
    n, inside, clear = region_flags(here_ref, cloud_ref)
    q_table = region(q, q_swap, None, q_off, q_cor, (own_twin, q_twin, None), n, (3, n, None))
    g_table = region(g, g_swap, None, g_off, g_cor, (g_twin, g_twin, None), 0, (0, 1, None))

    def finish(t, kt, fs, dk, dv):
        ksum_ref[t, :, fs] = dk
        vsum_ref[t, :, fs] = dv

    key_terms((inside, clear), (0, 1), k_ref, v_ref, n, q_table, g_table, rows_ref, finish)


def outer_near_kernel(here_ref, cloud_ref, k_ref, v_ref, ksum_ref, vsum_ref, *rest):
    q_far, g_far, kout_ref, vout_ref, rows_ref = rest
    n, inside, clear = region_flags(here_ref, cloud_ref)
    q_table = region(None, None, q_far, None, None, (None,) * 3, n, (None,) * 3)
    g_table = region(None, None, g_far, None, None, (None,) * 3, 0, (None,) * 3)

    def finish(t, kt, fs, dk, dv):
        kout_ref[:, fs] = ((ksum_ref[t, :, fs] + dk) * SCALE).astype(BF)
        vout_ref[:, fs] = (vsum_ref[t, :, fs] + dv).astype(BF)

    key_terms((inside, clear), (2,), k_ref, v_ref, n, q_table, g_table, rows_ref, finish, (0,))


def outer_face_kernel(here_ref, cloud_ref, k_ref, v_ref, ksum_ref, vsum_ref, *rest):
    q_far, q_twin, g_far, g_twin, k_near_ref, v_near_ref, kout_ref, vout_ref, rows_ref = rest
    n, inside, clear = region_flags(here_ref, cloud_ref)
    kout_ref[n] = k_near_ref[...]
    vout_ref[n] = v_near_ref[...]
    q_table = region(None, None, q_far, None, None, (None, None, q_twin), n, (n, n, n))
    g_table = region(None, None, g_far, None, None, (None, None, g_twin), 0, (1, 1, 1))

    def finish(t, kt, fs, dk, dv):
        kout_ref[kt, :, fs] = ((ksum_ref[t, :, fs] + dk) * SCALE).astype(BF)
        vout_ref[kt, :, fs] = (vsum_ref[t, :, fs] + dv).astype(BF)

    key_terms((inside, clear), (2,), k_ref, v_ref, n, q_table, g_table, rows_ref, finish, (1,))


SMEM = pl.BlockSpec(memory_space=pltpu.SMEM)
VMEM = pl.BlockSpec(memory_space=pltpu.VMEM)
ANY = pl.BlockSpec(memory_space=pl.ANY)


def call(kernel, name, in_specs, out_shape, scratch):
    return pl.pallas_call(
        kernel,
        name=name,
        out_shape=out_shape,
        in_specs=in_specs,
        out_specs=jax.tree.map(lambda _: VMEM, out_shape),
        scratch_shapes=scratch,
        compiler_params=pltpu.CompilerParams(vmem_limit_bytes=VMEM_LIMIT),
        cost_estimate=pl.CostEstimate(flops=1000, bytes_accessed=1000, transcendentals=0),
    )


def shape(dims, dtype):
    return jax.ShapeDtypeStruct(dims, dtype)


def body(way, queries, keys, values, season, cloud, pairing):
    lat = lax.axis_index("lat")
    lon = lax.axis_index("lon")
    q, k, v, s = (x[0] for x in (queries, keys, values, season))

    here = jnp.stack([lat, lon]).astype(jnp.int32)

    def move(x, kind):
        return lax.ppermute(x, AXES, way[kind])

    def named(name, x, kind):
        with jax.named_scope(name + "_" + kind):
            return move(x, kind)

    def joined(*parts):
        total = sum(p.shape[0] for p in parts)
        return call(
            functools.partial(join_kernel, len(parts)),
            "join",
            [VMEM] * len(parts),
            shape((total,) + parts[0].shape[1:], parts[0].dtype),
            [],
        )(*parts)

    k_swap = named("key", k, "swap")
    v_swap = named("value", v, "swap")
    edge, q_near, pair = call(
        edges_kernel,
        "edges",
        [SMEM, VMEM] + [ANY] * 4,
        (
            shape((3, PP, WIDTH), BF),
            shape((1, PP, WIDTH), BF),
            shape((2, PP), jnp.int32),
        ),
        [pltpu.SemaphoreType.DMA((4,))],
    )(here, pairing[0], k, v, s, q)
    k_swap, edge, s1 = phase(k_swap, edge, s)
    cor = named("kvs", edge, "cor")
    k_far = named("key", k_swap, "far")
    s_swap = named("season", s1, "swap")
    v_far = named("value", v_swap, "far")
    k_far, v_far, cor, s_swap, edge, q1, q_near = phase(k_far, v_far, cor, s_swap, edge, q, q_near)
    far_stack, faces = call(
        pack_kernel,
        "pack",
        [SMEM] + [VMEM] * 10,
        (shape((5, PP, WIDTH), BF), shape((9, PP, WIDTH), BF)),
        [],
    )(here, k, v, s, q, k_swap, v_swap, s_swap, k_far, v_far, cor)
    far = named("season", far_stack, "far")
    off = named("kvs", edge, "off")
    q_swap = named("query", q1, "swap")
    q_cor = named("query", q_near, "cor")
    twin = named("faces", faces, "twin")
    twin, q_cor, off, q_swap, far = phase(twin, q_cor, off, q_swap, far)
    far_twin = named("season_far", far, "twin")
    q_far = named("query", joined(q_swap, q_cor), "far")
    kvp = (k, v, k_swap, v_swap, k_far, v_far, far, cor, off, twin)

    att, stat = call(
        attend_kernel,
        "attend",
        [SMEM, SMEM, VMEM] + [VMEM] * 10,
        (shape((2, PP, WIDTH), BF), shape((2, PP, 128), F32)),
        [],
    )(here, cloud, q, *kvp)

    loss, grad, stats = call(
        contrast_kernel,
        "contrast",
        [SMEM, SMEM, VMEM, VMEM, VMEM] + [VMEM] * 7,
        (shape((2, PP), F32), shape((2, PP, EXT), BF), shape((2, PP, 128), F32)),
        [],
    )(here, cloud, att, stat, pair, s, s_swap, far, off, cor, twin, far_twin)

    g_near = grad[0:1]
    g_swap = named("grad", grad, "swap")
    g_cor = named("grad", g_near, "cor")
    g_off = named("grad", g_near, "off")
    query_grad = call(
        query_kernel,
        "query_grads",
        [SMEM, SMEM, VMEM, VMEM, VMEM] + [VMEM] * 10,
        shape((2, PP, WIDTH), BF),
        [],
    )(here, cloud, q, grad, stats, *kvp)

    q_off = named("query", after(q_near, grad), "off")
    g_swap, g_cor, g_off, q_off, q_far, query_grad, q_swap1 = phase(
        g_swap, g_cor, g_off, q_off, q_far, query_grad, q_swap
    )
    q_swap_twin = named("query", q_swap1, "twin")
    far_stack, faces = call(
        grad_pack_kernel,
        "grad_pack",
        [VMEM] * 3,
        (shape((3, PP, EXT), BF), shape((2, PP, EXT), BF)),
        [],
    )(grad, g_swap, g_cor)
    g_far = named("grad", far_stack, "far")
    g_twin = named("grad", faces, "twin")
    q_far_twin = named("query_far", q_far, "twin")

    key_sum, value_sum = call(
        inner_key_kernel,
        "inner_key_grads",
        [SMEM, SMEM, VMEM, VMEM] + [VMEM] * 11,
        (shape((2, PP, WIDTH), F32), shape((2, PP, WIDTH), F32)),
        [pltpu.VMEM((2 * HEADS, 6 * PP), F32)],
    )(
        here, cloud, k, v, q, q_swap, q_off, q_cor, twin, q_swap_twin,
        grad, g_swap, g_off, g_cor, g_twin,
    )

    g_far, q_far_twin, key_sum, value_sum = phase(g_far, q_far_twin, key_sum, value_sum)
    g_last = named("grad_last", g_far, "twin")
    k_near_grad, v_near_grad = call(
        outer_near_kernel,
        "outer_near_key_grads",
        [SMEM, SMEM] + [VMEM] * 6,
        (shape((PP, WIDTH), BF), shape((PP, WIDTH), BF)),
        [pltpu.VMEM((2 * HEADS, 3 * PP), F32)],
    )(here, cloud, k, v, key_sum, value_sum, q_far, g_far)
    key_grad, value_grad = call(
        outer_face_kernel,
        "outer_face_key_grads",
        [SMEM, SMEM] + [VMEM] * 10,
        (shape((2, PP, WIDTH), BF), shape((2, PP, WIDTH), BF)),
        [pltpu.VMEM((2 * HEADS, 3 * PP), F32)],
    )(
        here, cloud, k, v, key_sum, value_sum, q_far, q_far_twin, g_far, g_last,
        k_near_grad, v_near_grad,
    )

    return (loss[None], query_grad[None], key_grad[None], value_grad[None])


def solution(mesh):
    block = P("lat", "lon", None, None)
    line = P("lat", "lon", None)
    way = routes(mesh.shape["lat"], mesh.shape["lon"])
    return jax.shard_map(
        functools.partial(body, way),
        mesh=mesh,
        in_specs=(block, block, block, block, P(), line),
        out_specs=(line, block, block, block),
        check_vma=False,
    )
```

```python
import functools

import jax
import jax.numpy as jnp
from jax import lax
from jax.experimental import pallas as pl
from jax.experimental.pallas import tpu as pltpu
from jax.sharding import PartitionSpec as P

HEADS = 16
HDIM = 64
PP = 64
WIDTH = HEADS * HDIM
GROUP = 4
GW = GROUP * HDIM
GROUPS = HEADS // GROUP
ROWS = GROUP * PP
WIN = 9 * PP
REG = 12 * PP
EXT = WIDTH + 128
NEG_FILL = -1e30
SCALE = HDIM ** -0.5
AXES = ("lon", "lat")
VMEM_LIMIT = 48 * 1024 * 1024
BF = jnp.bfloat16
F32 = jnp.float32

NT = (((1,), (1,)), ((), ()))
NN = (((1,), (0,)), ((), ()))


def dot(a, b, dims):
    return lax.dot_general(a, b, dims, preferred_element_type=F32)


def routes(rows, cols):
    def at(r, c):
        return (c % cols) * rows + r

    cells = [(r, c) for r in range(rows) for c in range(cols)]

    def away(c):
        return c + 1 if c % 2 else c - 1

    def hop(r):
        return r + 2 if r % 2 == 0 else r - 2

    def past(r):
        return r - 1 if r % 2 == 0 else r + 1

    return dict(
        swap=[(at(r, c), at(r ^ 1, c)) for r, c in cells],
        off=[(at(r, c), at(r, away(c))) for r, c in cells],
        cor=[(at(r, c), at(r ^ 1, away(c))) for r, c in cells],
        far=[(at(r, c), at(hop(r), c)) for r, c in cells if 0 <= hop(r) < rows],
        twin=[(at(r, c), at(r, c ^ 1)) for r, c in cells],
        out=[(at(r, c), at(past(r), c)) for r, c in cells if 0 <= past(r) < rows],
        edge=[(at(r, c), at(past(r), away(c))) for r, c in cells if 0 <= past(r) < rows],
    )


def after(x, *done):
    return lax.optimization_barrier((x,) + done)[0]


def phase(*values):
    return lax.optimization_barrier(values)


def region(own, swap, far, off, cor, twins, n, inner):
    return (
        ((off, 0), (own, n), (own, 1 - n), (twins[0], inner[0])),
        ((cor, 0), (swap, n), (swap, 1 - n), (twins[1], inner[1])),
        ((far, 2), (far, n), (far, 1 - n), (twins[2], inner[2])),
    )


def window(table, t, fs, rows=(0, 1, 2)):
    places = [table[row][col + t] for row in rows for col in range(3)]
    return jnp.concatenate([ref[index, :, fs] for ref, index in places], axis=0)


def spread(x):
    lane = lax.broadcasted_iota(jnp.int32, x.shape, 1) // HDIM
    return jnp.concatenate([jnp.where(lane == h, x, jnp.zeros_like(x)) for h in range(GROUP)], axis=0)


def gather_heads(y):
    lane = lax.broadcasted_iota(jnp.int32, (PP, GW), 1) // HDIM
    out = y[0:PP]
    for h in range(1, GROUP):
        out = jnp.where(lane == h, y[h * PP : (h + 1) * PP], out)
    return out


def group_slice(g):
    return pl.ds(pl.multiple_of(g * GW, GW), GW)


def region_flags(here_ref, cloud_ref):
    rows, cols = cloud_ref.shape
    lat, lon = here_ref[0], here_ref[1]
    odd = lon % 2
    sign = 2 * odd - 1
    near = 2 * lon + odd
    outer = jnp.where(lat % 2 == 0, lat - 1, lat + 1)
    within = (outer >= 0) & (outer < rows)
    partner = jnp.where(lat % 2 == 0, lat + 1, lat - 1)
    lines = (lat, partner, jnp.clip(outer, 0, rows - 1))
    inside = (True, True, within)
    clear = []
    for row in range(3):
        line = []
        for col in range(4):
            c = (near + sign * (1 - col) + cols) % cols
            flag = cloud_ref[lines[row], c] == 1
            line.append(flag & within if row == 2 else flag)
        clear.append(line)
    return odd, inside, clear


def segments(flags, fill):
    width = PP * len(flags)
    slot = lax.broadcasted_iota(jnp.int32, (1, width), 1) // PP
    out = jnp.zeros((1, width), F32)
    for i, flag in enumerate(flags):
        if flag is not True:
            value = fill if flag is False else jnp.where(flag, 0.0, fill)
            out = jnp.where(slot == i, value, out)
    return out


def query_flags(clear, t):
    return [
        True if (row, col) == (0, 1) else clear[row][col + t] for row in range(3) for col in range(3)
    ]


def join_kernel(count, *refs):
    out = refs[count]
    at = 0
    for ref in refs[:count]:
        size = ref.shape[0]
        out[at : at + size] = ref[...]
        at += size


def edges_kernel(here_ref, pair_ref, k_ref, v_ref, s_ref, q_ref, off_ref, qn_ref, pair_out, sems):
    n = here_ref[1] % 2
    copies = [
        pltpu.make_async_copy(
            ref.at[n], off_ref.at[i] if i < 3 else qn_ref.at[0], sems.at[i]
        )
        for i, ref in enumerate((k_ref, v_ref, s_ref, q_ref))
    ]
    for c in copies:
        c.start()
    pair_out[...] = pair_ref[...]
    for c in copies:
        c.wait()


def pack_kernel(here_ref, k_ref, v_ref, s_ref, q_ref, ks_ref, vs_ref, ss_ref, kf_ref, vf_ref, cor_ref,
                far_ref, face_ref):
    n = here_ref[1] % 2
    far_ref[0:2] = ss_ref[...]
    far_ref[2:5] = cor_ref[...]
    for i, ref in enumerate((k_ref, v_ref, s_ref, q_ref, ks_ref, vs_ref, ss_ref, kf_ref, vf_ref)):
        face_ref[i] = ref[1 - n]


def grad_pack_kernel(grad_ref, swap_ref, cor_ref, far_ref, face_ref):
    far_ref[0:2] = swap_ref[...]
    far_ref[2] = cor_ref[0]
    face_ref[0] = grad_ref[1]
    face_ref[1] = swap_ref[1]


def key_value_tables(refs, n):
    k, v, k_swap, v_swap, k_far, v_far, far, cor, off, twin = refs
    return [
        (
            ((off, i), (own, n), (own, 1 - n), (twin, i)),
            ((cor, i), (swap, n), (swap, 1 - n), (twin, 4 + i)),
            ((far, 2 + i), (outer, n), (outer, 1 - n), (twin, 7 + i)),
        )
        for i, (own, swap, outer) in enumerate(((k, k_swap, k_far), (v, v_swap, v_far)))
    ]


def attend_kernel(here_ref, cloud_ref, q_ref, *rest):
    n, _, clear = region_flags(here_ref, cloud_ref)
    k_table, v_table = key_value_tables(rest[0:10], n)
    att_ref, stat_ref = rest[10:]
    for t in range(2):
        qt = n if t == 0 else 1 - n
        stat_ref[t] = jnp.zeros((PP, 128), F32)
        mask = segments(query_flags(clear, t), NEG_FILL)

        def step(g, carry):
            fs = group_slice(g)
            q = spread(q_ref[qt, :, fs] * SCALE)
            kw = window(k_table, t, fs)
            s = dot(q, kw, NT) + mask
            m = jnp.max(s, axis=1, keepdims=True)
            e = jnp.exp(s - m)
            total = jnp.sum(e, axis=1, keepdims=True)
            p = (e * (1.0 / total)).astype(BF)
            lse = m + jnp.log(total)
            att_ref[t, :, fs] = gather_heads(dot(p, window(v_table, t, fs), NN)).astype(BF)
            lane = lax.broadcasted_iota(jnp.int32, (PP, 128), 1)
            stat = stat_ref[t]
            for h in range(GROUP):
                stat = jnp.where(lane == g * GROUP + h, lse[h * PP : (h + 1) * PP], stat)
            stat_ref[t] = stat
            return carry

        lax.fori_loop(0, GROUPS, step, 0, unroll=True)


def contrast_kernel(here_ref, cloud_ref, att_ref, stat_ref, pair_ref, *rest):
    loss_ref, grad_ref, stats_ref = rest[7:]
    n, _, clear = region_flags(here_ref, cloud_ref)
    s, swap, far, off, cor, twin, far_twin = rest[0:7]
    table = (
        ((off, 2), (s, n), (s, 1 - n), (twin, 2)),
        ((cor, 2), (swap, n), (swap, 1 - n), (twin, 6)),
        ((far, 4), (far, n), (far, 1 - n), (far_twin, n)),
    )
    season = jnp.concatenate([ref[index] for line in table for ref, index in line], axis=0)
    att = jnp.concatenate([att_ref[0], att_ref[1]], axis=0)
    side = lax.broadcasted_iota(jnp.int32, (2 * PP, REG), 0) < PP
    sides = []
    for t in range(2):
        flags = query_flags(clear, t)
        line = []
        for row in range(3):
            mine = flags[row * 3 : row * 3 + 3]
            line += mine + [False] if t == 0 else [False] + mine
        sides.append(segments(line, NEG_FILL))
    mask = jnp.where(side, sides[0], sides[1])
    logits = dot(att, season, NT) + mask
    m = jnp.max(logits, axis=1, keepdims=True)
    e = jnp.exp(logits - m)
    total = jnp.sum(e, axis=1, keepdims=True)
    w = (e * (1.0 / total)).astype(BF)
    ctotal = m + jnp.log(total)
    key = lax.broadcasted_iota(jnp.int32, (4 * PP, PP), 0)
    hits = []
    for t in range(2):
        pair = pair_ref[pl.ds(n if t == 0 else 1 - n, 1), :]
        hits.append((key == pair + (1 + t) * PP).astype(F32))
    hit = jnp.transpose(jnp.concatenate(hits, axis=1)) > 0.5
    chosen = jnp.sum(jnp.where(hit, logits[:, 0 : 4 * PP], 0.0), axis=1, keepdims=True)
    loss = jnp.transpose(jnp.broadcast_to(ctotal - chosen, (2 * PP, 128)))
    for t in range(2):
        loss_ref[pl.ds(n if t == 0 else 1 - n, 1), :] = loss[0:1, t * PP : (t + 1) * PP]
    acc = dot(w, season, NN) - dot(hit.astype(F32).astype(BF), season[0 : 4 * PP], NN)
    grad = acc.astype(BF)
    prod = grad.astype(F32) * att.astype(F32)
    high = prod.astype(BF)
    low = (prod - high.astype(F32)).astype(BF)
    feat = lax.broadcasted_iota(jnp.int32, (WIDTH, 128), 0) // HDIM
    lane = lax.broadcasted_iota(jnp.int32, (WIDTH, 128), 1)
    pick = (lane == feat + HEADS).astype(F32).astype(BF)
    delta = dot(high, pick, NN) + dot(low, pick, NN)
    stat = jnp.concatenate([stat_ref[0], stat_ref[1]], axis=0) + delta
    part0 = stat.astype(BF).astype(F32)
    part1 = (stat - part0).astype(BF).astype(F32)
    part2 = (stat - part0 - part1).astype(BF).astype(F32)
    packed = part0 + pltpu.roll(part1, 32, 1) + pltpu.roll(part2, 64, 1)
    packed = packed.astype(BF)
    for t in range(2):
        rows = slice(t * PP, (t + 1) * PP)
        grad_ref[t, :, 0:WIDTH] = grad[rows]
        grad_ref[t, :, WIDTH:EXT] = packed[rows]
        stats_ref[t] = stat[rows]


def head_column(stat, index):
    lane = lax.broadcasted_iota(jnp.int32, (PP, 128), 1)
    cols = [
        jnp.sum(jnp.where(lane == index + h, stat, 0.0), axis=1, keepdims=True) for h in range(GROUP)
    ]
    return jnp.concatenate(cols, axis=0)


def query_kernel(here_ref, cloud_ref, q_ref, grad_ref, stats_ref, *rest):
    n, _, clear = region_flags(here_ref, cloud_ref)
    k_table, v_table = key_value_tables(rest[0:10], n)
    out_ref = rest[10]
    for t in range(2):
        qt = n if t == 0 else 1 - n
        mask = segments(query_flags(clear, t), NEG_FILL)

        def step(g, carry):
            fs = group_slice(g)
            q = spread(q_ref[qt, :, fs] * SCALE)
            stat = stats_ref[t]
            lse = head_column(stat, g * GROUP)
            delta = head_column(stat, g * GROUP + HEADS)
            kw = window(k_table, t, fs)
            s = dot(q, kw, NT) + mask
            p = jnp.exp(s - lse)
            gd = dot(spread(grad_ref[t, :, fs]), window(v_table, t, fs), NT)
            ds = (p * (gd - delta)).astype(BF)
            out = gather_heads(dot(ds, kw, NN)) * SCALE
            out_ref[qt, :, fs] = out.astype(BF)
            return carry

        lax.fori_loop(0, GROUPS, step, 0, unroll=True)


def key_terms(flags, rows, k_ref, v_ref, n, q_table, g_table, rows_ref, finish, blocks=(0, 1)):
    inside, clear = flags
    for t in blocks:
        kt = n if t == 0 else 1 - n
        parts = jnp.transpose(window(g_table, t, slice(WIDTH, EXT), rows).astype(F32))
        stats = parts[0:32] + parts[32:64] + parts[64:96]
        seen = clear[0][1 + t]
        open_to = [
            True if (row, col) == (0, 1) else (seen & inside[2] if row == 2 else seen)
            for row in rows
            for col in range(3)
        ]
        rows_ref[0:HEADS] = stats[0:HEADS] + segments(open_to, -NEG_FILL)
        rows_ref[HEADS : 2 * HEADS] = stats[HEADS : 2 * HEADS]

        def step(g, carry):
            fs = group_slice(g)
            ks = spread(k_ref[kt, :, fs] * SCALE)
            vs = spread(v_ref[kt, :, fs])
            qw = window(q_table, t, fs, rows)
            gw = window(g_table, t, fs, rows)
            s = dot(ks, qw, NT)
            gd = dot(vs, gw, NT)
            ps, dss = [], []
            for h in range(GROUP):
                part = slice(h * PP, (h + 1) * PP)
                lse = rows_ref[pl.ds(g * GROUP + h, 1), :]
                delta = rows_ref[pl.ds(HEADS + g * GROUP + h, 1), :]
                p = jnp.exp(s[part] - lse)
                ps.append(p.astype(BF))
                dss.append((p * (gd[part] - delta)).astype(BF))
            p = jnp.concatenate(ps, axis=0)
            ds = jnp.concatenate(dss, axis=0)
            finish(t, kt, fs, gather_heads(dot(ds, qw, NN)), gather_heads(dot(p, gw, NN)))
            return carry

        lax.fori_loop(0, GROUPS, step, 0, unroll=True)


def inner_key_kernel(here_ref, cloud_ref, k_ref, v_ref, *rest):
    q, q_swap, q_off, q_cor, own_twin, q_twin, g, g_swap, g_off, g_cor, g_twin = rest[0:11]
    ksum_ref, vsum_ref, rows_ref = rest[11:]
    n, inside, clear = region_flags(here_ref, cloud_ref)
    q_table = region(q, q_swap, None, q_off, q_cor, (own_twin, q_twin, None), n, (3, n, None))
    g_table = region(g, g_swap, None, g_off, g_cor, (g_twin, g_twin, None), 0, (0, 1, None))

    def finish(t, kt, fs, dk, dv):
        ksum_ref[t, :, fs] = dk
        vsum_ref[t, :, fs] = dv

    key_terms((inside, clear), (0, 1), k_ref, v_ref, n, q_table, g_table, rows_ref, finish)


def outer_near_kernel(here_ref, cloud_ref, k_ref, v_ref, ksum_ref, vsum_ref, *rest):
    q_far, g_far, kout_ref, vout_ref, rows_ref = rest
    n, inside, clear = region_flags(here_ref, cloud_ref)
    q_table = region(None, None, q_far, None, None, (None,) * 3, n, (None,) * 3)
    g_table = region(None, None, g_far, None, None, (None,) * 3, 0, (None,) * 3)

    def finish(t, kt, fs, dk, dv):
        kout_ref[:, fs] = ((ksum_ref[t, :, fs] + dk) * SCALE).astype(BF)
        vout_ref[:, fs] = (vsum_ref[t, :, fs] + dv).astype(BF)

    key_terms((inside, clear), (2,), k_ref, v_ref, n, q_table, g_table, rows_ref, finish, (0,))


def outer_face_kernel(here_ref, cloud_ref, k_ref, v_ref, ksum_ref, vsum_ref, *rest):
    q_far, q_twin, g_far, g_twin, k_near_ref, v_near_ref, kout_ref, vout_ref, rows_ref = rest
    n, inside, clear = region_flags(here_ref, cloud_ref)
    kout_ref[n] = k_near_ref[...]
    vout_ref[n] = v_near_ref[...]
    q_table = region(None, None, q_far, None, None, (None, None, q_twin), n, (n, n, n))
    g_table = region(None, None, g_far, None, None, (None, None, g_twin), 0, (1, 1, 1))

    def finish(t, kt, fs, dk, dv):
        kout_ref[kt, :, fs] = ((ksum_ref[t, :, fs] + dk) * SCALE).astype(BF)
        vout_ref[kt, :, fs] = (vsum_ref[t, :, fs] + dv).astype(BF)

    key_terms((inside, clear), (2,), k_ref, v_ref, n, q_table, g_table, rows_ref, finish, (1,))


SMEM = pl.BlockSpec(memory_space=pltpu.SMEM)
VMEM = pl.BlockSpec(memory_space=pltpu.VMEM)
ANY = pl.BlockSpec(memory_space=pl.ANY)


def call(kernel, name, in_specs, out_shape, scratch):
    return pl.pallas_call(
        kernel,
        name=name,
        out_shape=out_shape,
        in_specs=in_specs,
        out_specs=jax.tree.map(lambda _: VMEM, out_shape),
        scratch_shapes=scratch,
        compiler_params=pltpu.CompilerParams(vmem_limit_bytes=VMEM_LIMIT),
        cost_estimate=pl.CostEstimate(flops=1000, bytes_accessed=1000, transcendentals=0),
    )


def shape(dims, dtype):
    return jax.ShapeDtypeStruct(dims, dtype)


def body(way, queries, keys, values, season, cloud, pairing):
    lat = lax.axis_index("lat")
    lon = lax.axis_index("lon")
    q, k, v, s = (x[0] for x in (queries, keys, values, season))

    here = jnp.stack([lat, lon]).astype(jnp.int32)

    def move(x, kind):
        return lax.ppermute(x, AXES, way[kind])

    def named(name, x, kind):
        with jax.named_scope(name + "_" + kind):
            return move(x, kind)

    def joined(*parts):
        total = sum(p.shape[0] for p in parts)
        return call(
            functools.partial(join_kernel, len(parts)),
            "join",
            [VMEM] * len(parts),
            shape((total,) + parts[0].shape[1:], parts[0].dtype),
            [],
        )(*parts)

    k_swap = named("key", k, "swap")
    v_swap = named("value", v, "swap")
    edge, q_near, pair = call(
        edges_kernel,
        "edges",
        [SMEM, VMEM] + [ANY] * 4,
        (
            shape((3, PP, WIDTH), BF),
            shape((1, PP, WIDTH), BF),
            shape((2, PP), jnp.int32),
        ),
        [pltpu.SemaphoreType.DMA((4,))],
    )(here, pairing[0], k, v, s, q)
    k_swap, edge, s1 = phase(k_swap, edge, s)
    cor = named("kvs", edge, "cor")
    k_far = named("key", k_swap, "far")
    s_swap = named("season", s1, "swap")
    v_far = named("value", v_swap, "far")
    k_far, v_far, cor, s_swap, edge, q1, q_near = phase(k_far, v_far, cor, s_swap, edge, q, q_near)
    far_stack, faces = call(
        pack_kernel,
        "pack",
        [SMEM] + [VMEM] * 10,
        (shape((5, PP, WIDTH), BF), shape((9, PP, WIDTH), BF)),
        [],
    )(here, k, v, s, q, k_swap, v_swap, s_swap, k_far, v_far, cor)
    far = named("season", far_stack, "far")
    off = named("kvs", edge, "off")
    q_swap = named("query", q1, "swap")
    q_cor = named("query", q_near, "cor")
    twin = named("faces", faces, "twin")
    q_stack = joined(q_swap, q_cor)
    twin, q_cor, off, q_swap, q_stack, far = phase(twin, q_cor, off, q_swap, q_stack, far)
    far_twin = named("season_far", far, "twin")
    q_far = named("query", q_stack, "far")
    kvp = (k, v, k_swap, v_swap, k_far, v_far, far, cor, off, twin)

    att, stat = call(
        attend_kernel,
        "attend",
        [SMEM, SMEM, VMEM] + [VMEM] * 10,
        (shape((2, PP, WIDTH), BF), shape((2, PP, 128), F32)),
        [],
    )(here, cloud, q, *kvp)

    loss, grad, stats = call(
        contrast_kernel,
        "contrast",
        [SMEM, SMEM, VMEM, VMEM, VMEM] + [VMEM] * 7,
        (shape((2, PP), F32), shape((2, PP, EXT), BF), shape((2, PP, 128), F32)),
        [],
    )(here, cloud, att, stat, pair, s, s_swap, far, off, cor, twin, far_twin)

    g_near = grad[0:1]
    g_swap = named("grad", grad, "swap")
    g_cor = named("grad", g_near, "cor")
    g_off = named("grad", g_near, "off")
    query_grad = call(
        query_kernel,
        "query_grads",
        [SMEM, SMEM, VMEM, VMEM, VMEM] + [VMEM] * 10,
        shape((2, PP, WIDTH), BF),
        [],
    )(here, cloud, q, grad, stats, *kvp)

    q_off = named("query", after(q_near, grad), "off")
    g_swap, g_cor, g_off, q_off, q_far, query_grad, q_swap1 = phase(
        g_swap, g_cor, g_off, q_off, q_far, query_grad, q_swap
    )
    q_swap_twin = named("query", q_swap1, "twin")
    far_stack, faces = call(
        grad_pack_kernel,
        "grad_pack",
        [VMEM] * 3,
        (shape((3, PP, EXT), BF), shape((2, PP, EXT), BF)),
        [],
    )(grad, g_swap, g_cor)
    g_far = named("grad", far_stack, "far")
    g_twin = named("grad", faces, "twin")
    q_far_twin = named("query_far", q_far, "twin")

    key_sum, value_sum = call(
        inner_key_kernel,
        "inner_key_grads",
        [SMEM, SMEM, VMEM, VMEM] + [VMEM] * 11,
        (shape((2, PP, WIDTH), F32), shape((2, PP, WIDTH), F32)),
        [pltpu.VMEM((2 * HEADS, 6 * PP), F32)],
    )(
        here, cloud, k, v, q, q_swap, q_off, q_cor, twin, q_swap_twin,
        grad, g_swap, g_off, g_cor, g_twin,
    )

    g_far, q_far_twin, key_sum, value_sum = phase(g_far, q_far_twin, key_sum, value_sum)
    g_last = named("grad_last", g_far, "twin")
    k_near_grad, v_near_grad = call(
        outer_near_kernel,
        "outer_near_key_grads",
        [SMEM, SMEM] + [VMEM] * 6,
        (shape((PP, WIDTH), BF), shape((PP, WIDTH), BF)),
        [pltpu.VMEM((2 * HEADS, 3 * PP), F32)],
    )(here, cloud, k, v, key_sum, value_sum, q_far, g_far)
    key_grad, value_grad = call(
        outer_face_kernel,
        "outer_face_key_grads",
        [SMEM, SMEM] + [VMEM] * 10,
        (shape((2, PP, WIDTH), BF), shape((2, PP, WIDTH), BF)),
        [pltpu.VMEM((2 * HEADS, 3 * PP), F32)],
    )(
        here, cloud, k, v, key_sum, value_sum, q_far, q_far_twin, g_far, g_last,
        k_near_grad, v_near_grad,
    )

    return (loss[None], query_grad[None], key_grad[None], value_grad[None])


def solution(mesh):
    block = P("lat", "lon", None, None)
    line = P("lat", "lon", None)
    way = routes(mesh.shape["lat"], mesh.shape["lon"])
    return jax.shard_map(
        functools.partial(body, way),
        mesh=mesh,
        in_specs=(block, block, block, block, P(), line),
        out_specs=(line, block, block, block),
        check_vma=False,
    )
```
